32 devices in a mesh: wide: 8 (over y, x, core), narrow: 4 (over z).
Axes of the slice: x: 2, y: 2, z: 4, core: 2. Of those that a mesh axis runs over, the one named last changes fastest.
Arguments:
- hidden: bfloat16 [128, 4096], P('wide'), may hold values from -6 to 6
- conv_cache: bfloat16 [3, 8192, 128], P(None, ('wide', 'narrow')), may hold values from -6 to 6
- ssm_cache: bfloat16 [8192, 16, 128], P(('wide', 'narrow')), may hold values from -6 to 6
- mixer_gain: float32 [4096], replicated, may hold values from 0.1 to 1.9
- in_weight: bfloat16 [2, 8192, 4096], P(None, ('wide', 'narrow')), may hold values from -0.09375 to 0.09375
- conv_weight: float32 [4, 8192], P(None, ('wide', 'narrow')), may hold values from -3 to 3
- conv_bias: float32 [8192], P(('wide', 'narrow')), may hold values from -3 to 3
- select_weight: bfloat16 [8192, 288], P(('wide', 'narrow')), may hold values from -0.125 to 0.125
- step_gain: float32 [256], replicated, may hold values from 0.1 to 1.9
- step_weight: bfloat16 [8192, 256], P(('wide', 'narrow')), may hold values from -0.375 to 0.375
- step_bias: float32 [8192], P(('wide', 'narrow')), may hold values from -5 to -1
- decay_log: float32 [8192, 16], P(('wide', 'narrow')), may hold values from 0 to 2.8
- skip_gain: float32 [8192], P(('wide', 'narrow')), may hold values from 0.5 to 1.5
- out_weight: bfloat16 [8192, 4096], P(('wide', 'narrow')), may hold values from -0.125 to 0.125
- ffn_gain: float32 [4096], replicated, may hold values from 0.1 to 1.9
- gate_proj: bfloat16 [4096, 98304], P(None, ('wide', 'narrow')), may hold values from -0.09375 to 0.09375
- up_proj: bfloat16 [4096, 98304], P(None, ('wide', 'narrow')), may hold values from -0.09375 to 0.09375
- down_proj: bfloat16 [98304, 4096], P(('wide', 'narrow')), may hold values from -0.109375 to 0.109375
- route_experts: int32 [128, 2], P('wide'), may hold values from 0 to 7, all different within a row; in each aligned block of 16 rows (0 to 15, 16 to 31, ...) at most 10 rows name the same one
- route_share: float32 [128, 2], P('wide'), may hold values from 0.2 to 1
Outputs:
- layer_out: bfloat16 [128, 4096], P('wide', 'narrow')
- new_state: bfloat16 [8192, 16, 128], P(('wide', 'narrow'))
The draws below stay inside these ranges and needn't reach their ends.
Inputs may be any that keep to these rules, and one draw needn't show every extreme that they name: `route_experts`: each row names two different experts. Among the 16 rows of one index of wide (aligned blocks), no expert is named by more than 10 rows, and in every draw some block has an expert named by exactly 10 rows.
All inputs are finite; a program needn't handle non-finite values.
Results may differ from the reference program's by a relative error of at most 0.017.
Values may be sent and summed in bfloat16 or wider, within the bound.
No kernel may reach another device: no remote copies, remote signals or barrier semaphores. Data moves between devices by JAX's collectives and lax.ppermute only.
A program may use at most 128 MiB of HBM per device.

```python
import math
import jax
import jax.numpy as jnp
import numpy as np
from jax import lax

D = 4096
DI = 8192
DS = 16
DTR = 256
EXPERTS = 8
FF = 12288
TOPK = 2
ROWS_DEV = 16
CAPACITY = 10
ROWS = 128
N_WIDE = 8


def with_spikes(values, key, source, target, shards_of, factor):
    owner, partner = [(jnp.arange(values.shape[position]) // (values.shape[position] // shards_of)).reshape([-1 if axis == position else 1 for axis in range(values.ndim)]) for position in (source, target)]
    chosen = jax.random.permutation(key, shards_of)[partner]
    strong = (owner == chosen) | (owner == (partner + shards_of // 2) % shards_of)
    return jnp.where(strong, factor * values, values)


def steps_of(rng, dims, cuts, least, largest):
    factor_of, own = 1.0, jax.random.fold_in(rng, 6)
    for position, parts in cuts:
        heights = jnp.exp(jax.random.uniform(jax.random.fold_in(own, position), (parts,), jnp.float32, least / len(cuts), largest / len(cuts)))
        factor_of = factor_of * jnp.repeat(heights, dims[position] // parts).reshape([-1 if axis == position else 1 for axis in range(len(dims))])
    return factor_of


def deal_out(rng, own, number, rows, number_of, top, bound, slope):
    sequence = jax.random.permutation(rng, number_of)
    crowded, usual = portions_of(number_of, rows * top, bound, slope, True), portions_of(number_of, rows * top, bound, slope, False)
    places = jnp.arange(number_of)

    def named(sizes, offset_by):
        used = int((sizes > 0).sum())
        fixed = max(1, used // 4)
        moved = fixed + (places - fixed + offset_by * (used - fixed)) % max(1, number_of - fixed)
        return jnp.zeros((number_of,), jnp.int32).at[sequence[jnp.where(places < fixed, places, moved)]].set(jnp.asarray(sizes, jnp.int32))

    sizes = jnp.where(number % 4 == 0, named(crowded, number // 4), named(usual, number - number // 4 - 1))
    mixed = jax.random.permutation(jax.random.fold_in(own, 3), number_of)
    donor, sink = mixed[0:number_of // 2 * 2:2], mixed[1:number_of // 2 * 2:2]
    margin = jnp.minimum(sizes[donor] - 1, bound - sizes[sink]) // 2
    margin = jnp.where((donor == sequence[0]) | (sink == sequence[0]) | (sizes[sink] == 0), 0, jnp.maximum(margin, 0))
    moved = jax.random.randint(jax.random.fold_in(own, 4), (number_of // 2,), 0, 1 << 20) % (margin + 1)
    sizes = sizes.at[donor].add(-moved).at[sink].add(moved)
    items = jnp.searchsorted(jnp.cumsum(sizes), jnp.arange(rows * top), side="right").astype(jnp.int32)
    listing = items.reshape(top, rows).T
    listing = listing[jax.random.permutation(jax.random.fold_in(own, 1), rows)]
    offset_by = jax.random.randint(jax.random.fold_in(own, 2), (rows, 1), 0, top)
    return jnp.take_along_axis(listing, (jnp.arange(top)[None, :] + offset_by) % top, axis=1)


def portions_of(number_of, total, bound, slope, full):
    portions = [(1 << 20) // math.isqrt(grade ** slope) + 1 for grade in range(1, number_of + 1)]
    largest = bound if full else min(bound, max(-(-total // number_of), total * portions[0] // sum(portions)))
    least = 1 if total - largest >= number_of - 1 else 0
    counts, rest = [largest] + [least] * (number_of - 1), total - largest - least * (number_of - 1)
    while rest > 0:
        free = [i for i in range(1, number_of) if counts[i] < largest] or [i for i in range(1, number_of) if counts[i] < bound]
        mass, budget = sum([portions[i] for i in free]), rest
        for i in free:
            addition = min(bound - counts[i], max(1, budget * portions[i] // mass), rest)
            counts[i] = counts[i] + addition
            rest = rest - addition
    return np.array(counts)


def noise(key, extent, deviation, limit, pieces=(), kind=jnp.bfloat16):
    array = deviation * jax.random.normal(key, extent, jnp.float32)
    if pieces:
        array = array * steps_of(key, extent, pieces, -0.22, 0.18)
    return jnp.clip(array, -limit, limit).astype(kind)


def heavy_noise(rng, extent, width, reach, shards, heavy, kind=jnp.bfloat16):
    values = width * jax.random.normal(rng, extent, jnp.float32)
    if shards:
        values = values * steps_of(rng, extent, shards, -0.22, 0.18)
    return jnp.clip(with_spikes(values, jax.random.fold_in(rng, 3), *heavy), -reach, reach).astype(kind)


def setup_inputs(seed: int = 0) -> dict:
    arg_keys = jax.random.split(jax.random.key(seed), 21)
    hidden = noise(arg_keys[0], (ROWS, D), 1.0, 6.0, ((0, 8),))
    conv_cache = noise(arg_keys[1], (3, DI, ROWS), 1.0, 6.0, ((1, 32),))
    ssm_cache = noise(arg_keys[2], (DI, DS, ROWS), 1.0, 6.0, ((0, 32),))
    mixer_gain = jnp.clip(1.0 + 0.18 * jax.random.normal(arg_keys[3], (D,), jnp.float32), 0.1, 1.9)
    in_weight = noise(arg_keys[4], (2, DI, D), D ** -0.5, 0.09375, ((1, 32),))
    conv_weight = noise(arg_keys[5], (4, DI), 4 ** -0.5, 3.0, ((1, 32),), jnp.float32)
    conv_bias = noise(arg_keys[6], (DI,), 0.5, 3.0, ((0, 32),), jnp.float32)
    select_weight = heavy_noise(arg_keys[7], (DI, DTR + 2 * DS), DI ** -0.5, 0.125, ((0, 32),), (0, 1, 32, 2.75))
    step_gain = jnp.clip(1.0 + 0.18 * jax.random.normal(arg_keys[8], (DTR,), jnp.float32), 0.1, 1.9)
    step_weight = noise(arg_keys[9], (DI, DTR), DTR ** -0.5, 0.375, ((0, 32),))
    step_bias = jnp.clip(-5.0 + 4.0 * jax.random.uniform(arg_keys[10], (DI,), jnp.float32) ** steps_of(arg_keys[10], (DI,), ((0, 32),), -0.2, 0.2), -5.0, -1.0)
    decay_log = jnp.clip(2.8 * jax.random.uniform(arg_keys[11], (DI, DS), jnp.float32) ** steps_of(arg_keys[11], (DI, DS), ((0, 32),), -0.2, 0.2), 0.0, 2.8)
    skip_gain = jnp.clip(0.5 + 1.0 * jax.random.uniform(arg_keys[12], (DI,), jnp.float32) ** steps_of(arg_keys[12], (DI,), ((0, 32),), -0.2, 0.2), 0.5, 1.5)
    out_weight = heavy_noise(arg_keys[13], (DI, D), DI ** -0.5, 0.125, ((0, 32),), (0, 1, 32, 2.75))
    ffn_gain = jnp.clip(1.0 + 0.18 * jax.random.normal(arg_keys[14], (D,), jnp.float32), 0.1, 1.9)
    gate_proj = noise(arg_keys[15], (D, EXPERTS * FF), D ** -0.5, 0.09375, ((1, 32),))
    up_proj = noise(arg_keys[16], (D, EXPERTS * FF), D ** -0.5, 0.09375, ((1, 32),))
    down_proj = heavy_noise(arg_keys[17], (EXPERTS * FF, D), FF ** -0.5, 0.109375, ((0, 32),), (0, 1, 32, 2.75))
    route_experts_keys = jax.random.split(jax.random.fold_in(arg_keys[18], 1), ROWS // ROWS_DEV)
    route_experts_turns = jax.random.permutation(jax.random.fold_in(arg_keys[18], 3), ROWS // ROWS_DEV)
    route_experts = jax.vmap(lambda own, number: deal_out(jax.random.fold_in(arg_keys[18], 2), own, number, ROWS_DEV, EXPERTS, TOPK, CAPACITY, 2))(route_experts_keys, route_experts_turns).reshape((ROWS, TOPK))
    route_share = jnp.clip(0.2 + 0.8 * jax.random.uniform(arg_keys[19], (ROWS, TOPK), jnp.float32) ** steps_of(arg_keys[19], (ROWS, TOPK), ((0, 8),), -0.2, 0.2), 0.2, 1.0)
    return {"hidden": hidden, "conv_cache": conv_cache, "ssm_cache": ssm_cache, "mixer_gain": mixer_gain, "in_weight": in_weight, "conv_weight": conv_weight, "conv_bias": conv_bias, "select_weight": select_weight, "step_gain": step_gain, "step_weight": step_weight, "step_bias": step_bias, "decay_log": decay_log, "skip_gain": skip_gain, "out_weight": out_weight, "ffn_gain": ffn_gain, "gate_proj": gate_proj, "up_proj": up_proj, "down_proj": down_proj, "route_experts": route_experts, "route_share": route_share}


def rms_scale(values, gain):
    mean_square = lax.optimization_barrier(jnp.mean(values * values, axis=-1, keepdims=True))
    return values * lax.rsqrt(mean_square + 1e-06) * gain

def reference(hidden, conv_cache, ssm_cache, mixer_gain, in_weight, conv_weight, conv_bias, select_weight, step_gain, step_weight, step_bias, decay_log, skip_gain, out_weight, ffn_gain, gate_proj, up_proj, down_proj, route_experts, route_share):
    hidden_f = hidden.astype(jnp.float32)
    normed = rms_scale(hidden_f, mixer_gain).astype(jnp.bfloat16)
    projected = jnp.einsum('kcd,rd->kcr', in_weight.astype(jnp.float32), normed.astype(jnp.float32))
    x_input = projected[0]
    z_gate = projected[1]
    history = conv_cache.astype(jnp.float32)
    pre_conv = conv_bias[:, None] + conv_weight[3][:, None] * x_input
    for tap in range(3):
        pre_conv = pre_conv + conv_weight[tap][:, None] * history[tap]
    conved = jax.nn.silu(pre_conv)
    conved_bf = conved.astype(jnp.bfloat16)
    selected = jnp.dot(conved_bf.T, select_weight, preferred_element_type=jnp.float32)
    step_low = rms_scale(selected[:, :DTR], step_gain).astype(jnp.bfloat16)
    step_size = jax.nn.softplus(jnp.dot(step_weight, step_low.T, preferred_element_type=jnp.float32) + step_bias[:, None])
    in_coef = selected[:, DTR:DTR + DS].T
    out_coef = selected[:, DTR + DS:].T
    decay = jnp.exp(-step_size[:, None, :] * jnp.exp(decay_log)[:, :, None])
    state_f = decay * ssm_cache.astype(jnp.float32) + (step_size * conved)[:, None, :] * in_coef[None, :, :]
    gated = ((lax.optimization_barrier(jnp.sum(state_f * out_coef[None, :, :], axis=1)) + skip_gain[:, None] * conved) * jax.nn.silu(z_gate)).astype(jnp.bfloat16)
    mixer_sum = jnp.dot(gated.T, out_weight, preferred_element_type=jnp.float32)
    residual = (hidden_f + mixer_sum).astype(jnp.bfloat16)
    residual_f = residual.astype(jnp.float32)
    ffn_in = rms_scale(residual_f, ffn_gain).astype(jnp.bfloat16)
    assign = route_experts.reshape(N_WIDE, ROWS_DEV * TOPK).astype(jnp.int32)
    hits = (assign[:, :, None] == jnp.arange(EXPERTS, dtype=jnp.int32)[None, None, :]).astype(jnp.int32)
    earlier = jnp.cumsum(hits, axis=1) - hits
    slot = lax.optimization_barrier(jnp.sum(earlier * hits, axis=2))
    target = assign * CAPACITY + slot
    placer = (jnp.arange(EXPERTS * CAPACITY, dtype=jnp.int32)[None, :, None] == target[:, None, :]).astype(jnp.float32)
    repeated = jnp.repeat(ffn_in.reshape(N_WIDE, ROWS_DEV, D), TOPK, axis=1).astype(jnp.float32)
    packed = jnp.einsum('wsa,wad->wsd', placer, repeated).astype(jnp.bfloat16)
    per_expert = packed.reshape(N_WIDE, EXPERTS, CAPACITY, D).transpose(1, 0, 2, 3).reshape(EXPERTS, N_WIDE * CAPACITY, D)

    def run_expert(item):
        index, arrived = item
        gate_slice = lax.dynamic_slice_in_dim(gate_proj, index * FF, FF, 1)
        up_slice = lax.dynamic_slice_in_dim(up_proj, index * FF, FF, 1)
        down_slice = lax.dynamic_slice_in_dim(down_proj, index * FF, FF, 0)
        gate_act = jnp.dot(arrived, gate_slice, preferred_element_type=jnp.float32)
        up_act = jnp.dot(arrived, up_slice, preferred_element_type=jnp.float32)
        inner = (jax.nn.silu(gate_act) * up_act).astype(jnp.bfloat16)
        return jnp.dot(inner, down_slice, preferred_element_type=jnp.float32)
    expert_out = lax.map(run_expert, (jnp.arange(EXPERTS, dtype=jnp.int32), per_expert))
    expert_out = expert_out.reshape(EXPERTS, N_WIDE, CAPACITY, D).transpose(1, 0, 2, 3).reshape(N_WIDE, EXPERTS * CAPACITY, D)
    weighted = (placer * route_share.reshape(N_WIDE, 1, ROWS_DEV * TOPK)).reshape(N_WIDE, EXPERTS * CAPACITY, ROWS_DEV, TOPK).sum(axis=3)
    ffn_sum = jnp.einsum('wsr,wsd->wrd', weighted, expert_out, precision=lax.Precision.HIGHEST).reshape(ROWS, D)
    layer_out = (residual_f + ffn_sum).astype(jnp.bfloat16)
    return (layer_out, state_f.astype(jnp.bfloat16))
```

```python
import functools

import jax
import jax.numpy as jnp
from jax import lax
from jax.experimental import pallas as pl
from jax.experimental.pallas import tpu as pltpu
from jax.sharding import PartitionSpec as P

EXPERTS = 8
EPS = 1e-06
MIB = 1 << 20
LANES = 128
F32 = jnp.float32
BF16 = jnp.bfloat16


def f32(values):
    return values.astype(F32)


def kernel_call(body, outs, args, scalars=1, scratch=(), limit=32):
    smem = pl.BlockSpec(memory_space=pltpu.SMEM)
    vmem = pl.BlockSpec(memory_space=pltpu.VMEM)
    return pl.pallas_call(
        body,
        out_shape=[jax.ShapeDtypeStruct(shape, dtype) for shape, dtype in outs],
        in_specs=[smem] * scalars + [vmem] * (len(args) - scalars),
        out_specs=[vmem] * len(outs),
        scratch_shapes=scratch,
        compiler_params=pltpu.CompilerParams(vmem_limit_bytes=limit * MIB),
    )(*args)


def normalized(block, gain):
    values = f32(block)
    mean_square = jnp.mean(values * values, axis=-1, keepdims=True)
    return (values * lax.rsqrt(mean_square + EPS) * gain).astype(BF16)


def sigmoid_times(values):
    return values / (1.0 + jnp.exp(-values))


def project_kernel(
    blocks,
    place,
    *refs,
):
    rows = refs[:blocks]
    gain, weight, cache, columns, select, conved_out, gate_out, keep, send, normed, selected = refs[
        blocks:
    ]
    me = place[0]
    count = rows[0].shape[0]
    for j in range(blocks):
        start = pl.multiple_of((me ^ j) * count, count)
        normed[pl.ds(start, count), :] = normalized(rows[j][...], gain[...])
    dims = (((1,), (1,)), ((), ()))
    x_input = lax.dot_general(weight[0], normed[...], dims, preferred_element_type=F32)
    pre_conv = columns[:, 4:5] + columns[:, 3:4] * x_input
    for tap in range(3):
        pre_conv = pre_conv + columns[:, tap : tap + 1] * f32(cache[tap])
    conved = sigmoid_times(pre_conv)
    conved_out[...] = conved
    selected[...] = jnp.dot(select[...], conved.astype(BF16), preferred_element_type=F32)
    half = keep.shape[0]
    side = me & 1
    keep[...] = selected[pl.ds(pl.multiple_of(side * half, 16), half), :].astype(BF16)
    send[...] = selected[pl.ds(pl.multiple_of((1 - side) * half, 16), half), :].astype(BF16)
    z_gate = lax.dot_general(weight[1], normed[...], dims, preferred_element_type=F32)
    gate_out[...] = sigmoid_times(z_gate)


def state_kernel(
    blocks,
    place,
    own_half,
    other_half,
    step_gain,
    step_weight,
    columns,
    conved,
    gate,
    cache,
    rates,
    out_weight,
    new_state,
    keep,
    send,
    selected,
    step,
    driven,
    mixed,
    turned,
):
    me = place[0]
    side = me & 1
    half = own_half.shape[0]
    channels, states, rows = cache.shape
    rank = step_weight.shape[1]
    count = rows // blocks
    selected[pl.ds(pl.multiple_of(side * half, 16), half), :] = f32(own_half[...])
    selected[pl.ds(pl.multiple_of((1 - side) * half, 16), half), :] = f32(other_half[...])
    low = selected[:rank, :]
    mean_square = jnp.mean(low * low, axis=0, keepdims=True)
    step_low = (low * lax.rsqrt(mean_square + EPS) * step_gain[...]).astype(BF16)
    raw = jnp.dot(step_weight[...], step_low, preferred_element_type=F32) + columns[:, 5:6]
    sizes = jnp.maximum(raw, 0.0) + jnp.log1p(jnp.exp(-jnp.abs(raw)))
    step[...] = sizes
    driven[...] = sizes * conved[...]
    in_coef = selected[rank : rank + states, :]
    out_coef = selected[rank + states :, :]

    def channel(c, carry):
        one = pl.ds(c, 1)
        state = jnp.exp(step[one, :] * rates[c]) * f32(cache[c]) + driven[one, :] * in_coef
        new_state[c] = state.astype(BF16)
        mixed[one, :] = jnp.sum(state * out_coef, axis=0, keepdims=True)
        return carry

    lax.fori_loop(0, channels, channel, 0, unroll=8)
    gated = (mixed[...] + columns[:, 6:7] * conved[...]) * gate[...]
    turned[...] = gated.T
    parts = []
    for side_of in range(2):
        for k in range(blocks // 2):
            start = pl.multiple_of((me ^ (2 * k + side_of)) * count, count)
            parts.append(turned[pl.ds(start, count), :].astype(BF16))
    left = jnp.concatenate(parts, axis=0)
    kept = keep.shape[0]
    width = out_weight.shape[1]
    piece = 512 if width % 512 == 0 else width
    for start in range(0, width, piece):
        span = slice(start, start + piece)
        partial = jnp.dot(left, out_weight[:, span], preferred_element_type=F32).astype(BF16)
        keep[:, span] = partial[:kept]
        send[:, span] = partial[kept:]


def split_kernel(keep, got, *outs):
    count = outs[0].shape[0]
    for k, out in enumerate(outs):
        span = slice(k * count, (k + 1) * count)
        out[...] = (f32(keep[span, :]) + f32(got[span, :])).astype(BF16)


def add_kernel(*refs):
    total = f32(refs[0][...])
    for ref in refs[1:-1]:
        total = total + f32(ref[...])
    refs[-1][...] = total.astype(refs[-1].dtype)


def residual_kernel(mine, got, hidden, experts, share, out):
    width = hidden.shape[1]
    residual = f32(hidden[...]) + (f32(mine[...]) + f32(got[...]))
    out[:, :width] = residual.astype(BF16)
    lane = lax.broadcasted_iota(jnp.int32, (hidden.shape[0], LANES), 1)
    first = lane < LANES // 2
    number = jnp.where(first, lane, lane - LANES // 2)
    dense = jnp.zeros(lane.shape, F32)
    for k in range(experts.shape[1]):
        dense = dense + jnp.where(number == experts[:, k : k + 1], share[:, k : k + 1], 0.0)
    upper = dense.astype(BF16)
    lower = (dense - f32(upper)).astype(BF16)
    out[:, width:] = jnp.where(first, f32(upper), f32(lower)).astype(BF16)


def expert_kernel(blocks, group, place, *refs):
    rows = refs[:blocks]
    gain, gate_proj, up_proj, down_proj, keep, send, normed, share, total = refs[blocks:]
    index = pl.program_id(0)
    count = rows[0].shape[0]
    width = gain.shape[1]

    @pl.when(index == 0)
    def _():
        expert = place[0] // group
        lane = lax.broadcasted_iota(jnp.int32, (count, LANES), 1)
        wanted = (lane == expert) | (lane == expert + LANES // 2)
        for j in range(blocks):
            span = slice(j * count, (j + 1) * count)
            normed[span, :] = normalized(rows[j][:, :width], gain[...])
            shares = jnp.where(wanted, f32(rows[j][:, width:]), 0.0)
            share[span, :] = jnp.broadcast_to(
                jnp.sum(shares, axis=1, keepdims=True), (count, LANES)
            )

    inputs = normed[...]
    gate_act = jnp.dot(inputs, gate_proj[...], preferred_element_type=F32)
    up_act = jnp.dot(inputs, up_proj[...], preferred_element_type=F32)
    inner = (sigmoid_times(gate_act) * up_act).astype(BF16)
    added = jnp.dot(inner, down_proj[...], preferred_element_type=F32)

    @pl.when(index == 0)
    def _():
        total[...] = added

    @pl.when(index > 0)
    def _():
        total[...] += added

    @pl.when(index == pl.num_programs(0) - 1)
    def _():
        weighted = (total[...] * share[:, :1]).astype(BF16)
        kept = keep.shape[0]
        keep[...] = weighted[:kept]
        send[...] = weighted[kept:]


def columns_kernel(place, *refs):
    outs = refs[-place_count(refs) :]
    ins = refs[: -len(outs)]
    size = outs[0].shape[1]
    me = place[1]
    for k, out in enumerate(outs):
        span = pl.ds(pl.multiple_of((me ^ k) * size, size), size)
        total = f32(ins[0][:, span])
        for ref in ins[1:]:
            total = total + f32(ref[:, span])
        out[...] = total.astype(BF16)


def place_count(refs):
    return refs[0].shape[1] // refs[-1].shape[1]


def final_kernel(place, residual, *refs):
    out = refs[-1]
    size = out.shape[1]
    span = pl.ds(pl.multiple_of(place[1] * size, size), size)
    total = f32(refs[0][...])
    for ref in refs[1:-1]:
        total = total + f32(ref[...])
    out[...] = (f32(residual[:, span]) + total).astype(BF16)


def on_device(
    hidden,
    conv_cache,
    ssm_cache,
    mixer_gain,
    in_weight,
    conv_weight,
    conv_bias,
    select_weight,
    step_gain,
    step_weight,
    step_bias,
    decay_log,
    skip_gain,
    out_weight,
    ffn_gain,
    gate_proj,
    up_proj,
    down_proj,
    route_experts,
    route_share,
):
    narrow_count = lax.axis_size("narrow")
    wide_count = lax.axis_size("wide")
    chips = wide_count // 2
    count, width = hidden.shape
    rows = count * wide_count
    channels, states = decay_log.shape
    chosen = select_weight.shape[1]
    hidden_units = gate_proj.shape[1]

    def swap(values):
        return lax.ppermute(values, "wide", [(i, i ^ 1) for i in range(wide_count)])

    def to_chip(values, k):
        return lax.ppermute(values, "wide", [(i, i ^ (2 * k)) for i in range(wide_count)])

    def to_narrow(values, k):
        return lax.ppermute(values, "narrow", [(i, i ^ k) for i in range(narrow_count)])

    def plane_gather(block):
        same = [block] + [to_chip(block, k) for k in range(1, chips)]
        other = [swap(item) for item in same]
        return same, other

    def plane_scatter(keep, got):
        parts = kernel_call(split_kernel, [((count, width), BF16)] * chips, (keep, got), scalars=0)
        return [parts[0]] + [to_chip(parts[k], k) for k in range(1, chips)]

    def add(*items):
        return kernel_call(add_kernel, [(items[0].shape, BF16)], items, scalars=0)[0]

    place = jnp.stack([lax.axis_index("wide"), lax.axis_index("narrow")]).astype(jnp.int32)
    columns = jnp.concatenate(
        [conv_weight.T, jnp.stack([conv_bias, step_bias, skip_gain], axis=1)], axis=1
    )
    rates = jnp.broadcast_to(-jnp.exp(decay_log)[:, :, None], (channels, states, rows))

    same, other = plane_gather(hidden)
    interleaved = [item for pair in zip(same, other) for item in pair]
    half = chosen // 2
    conved, gate, keep, send = kernel_call(
        functools.partial(project_kernel, wide_count),
        [
            ((channels, rows), F32),
            ((channels, rows), F32),
            ((half, rows), BF16),
            ((half, rows), BF16),
        ],
        (place, *interleaved, mixer_gain[None, :], in_weight, conv_cache, columns, select_weight.T),
        scratch=[pltpu.VMEM((rows, width), BF16), pltpu.VMEM((chosen, rows), F32)],
    )
    part = add(keep, swap(send))
    part = add(part, *[to_chip(part, k) for k in range(1, chips)])
    part = add(part, *[to_narrow(part, k) for k in range(1, narrow_count)])
    new_state, keep, send = kernel_call(
        functools.partial(state_kernel, wide_count),
        [
            (ssm_cache.shape, BF16),
            ((rows // 2, width), BF16),
            ((rows // 2, width), BF16),
        ],
        (
            place,
            part,
            swap(part),
            step_gain[:, None],
            step_weight,
            columns,
            conved,
            gate,
            ssm_cache,
            rates,
            out_weight,
        ),
        scratch=[
            pltpu.VMEM((chosen, rows), F32),
            pltpu.VMEM((channels, rows), F32),
            pltpu.VMEM((channels, rows), F32),
            pltpu.VMEM((channels, rows), F32),
            pltpu.VMEM((rows, channels), F32),
        ],
    )
    parts = plane_scatter(keep, swap(send))
    mine = add(*parts)
    step = 1
    while 2 * step < narrow_count:
        mine = add(mine, to_narrow(mine, step))
        step *= 2
    (residual,) = kernel_call(
        residual_kernel,
        [((count, width + LANES), BF16)],
        (mine, to_narrow(mine, step), hidden, route_experts, route_share),
        scalars=0,
    )
    same, other = plane_gather(residual)
    block = next(size for size in (256, 128, hidden_units) if hidden_units % size == 0)
    whole = pl.BlockSpec(memory_space=pltpu.VMEM)
    keep, send = pl.pallas_call(
        functools.partial(expert_kernel, wide_count, wide_count // EXPERTS),
        grid=(hidden_units // block,),
        out_shape=[jax.ShapeDtypeStruct((rows // 2, width), BF16)] * 2,
        in_specs=[pl.BlockSpec(memory_space=pltpu.SMEM)]
        + [whole] * (wide_count + 1)
        + [pl.BlockSpec((width, block), lambda i: (0, i))] * 2
        + [pl.BlockSpec((block, width), lambda i: (i, 0))],
        out_specs=[whole] * 2,
        scratch_shapes=[
            pltpu.VMEM((rows, width), BF16),
            pltpu.VMEM((rows, LANES), F32),
            pltpu.VMEM((rows, width), F32),
        ],
        compiler_params=pltpu.CompilerParams(vmem_limit_bytes=48 * MIB),
    )(place, *same, *other, ffn_gain[None, :], gate_proj, up_proj, down_proj)
    parts = plane_scatter(keep, swap(send))
    col_share = width // narrow_count
    shares = kernel_call(
        columns_kernel, [((count, col_share), BF16)] * narrow_count, (place, *parts)
    )
    (layer_out,) = kernel_call(
        final_kernel,
        [((count, col_share), BF16)],
        (
            place,
            residual,
            shares[0],
            *[to_narrow(shares[k], k) for k in range(1, narrow_count)],
        ),
    )
    return (layer_out, new_state)


def solution(mesh):
    placed = (
        P("wide", None),
        P(None, ("wide", "narrow"), None),
        P(("wide", "narrow"), None, None),
        P(),
        P(None, ("wide", "narrow"), None),
        P(None, ("wide", "narrow")),
        P(("wide", "narrow")),
        P(("wide", "narrow"), None),
        P(),
        P(("wide", "narrow"), None),
        P(("wide", "narrow")),
        P(("wide", "narrow"), None),
        P(("wide", "narrow")),
        P(("wide", "narrow"), None),
        P(),
        P(None, ("wide", "narrow")),
        P(None, ("wide", "narrow")),
        P(("wide", "narrow"), None),
        P("wide", None),
        P("wide", None),
    )
    return jax.shard_map(
        on_device,
        mesh=mesh,
        in_specs=placed,
        out_specs=(P("wide", "narrow"), P(("wide", "narrow"), None, None)),
        check_vma=False,
    )
```

```python
import functools

import jax
import jax.numpy as jnp
from jax import lax
from jax.experimental import pallas as pl
from jax.experimental.pallas import tpu as pltpu
from jax.sharding import PartitionSpec as P

EXPERTS = 8
EPS = 1e-06
MIB = 1 << 20
LANES = 128
PIECES = 4
F32 = jnp.float32
BF16 = jnp.bfloat16


def f32(values):
    return values.astype(F32)


def kernel_call(body, outs, args, scalars=1, far=0, scratch=(), limit=16, cost=None):
    smem = pl.BlockSpec(memory_space=pltpu.SMEM)
    vmem = pl.BlockSpec(memory_space=pltpu.VMEM)
    hbm = pl.BlockSpec(memory_space=pltpu.HBM)
    near = len(args) - far
    stay = [pltpu.with_memory_space_constraint(item, pltpu.HBM) for item in args[near:]]
    args = (*args[:near], *stay)
    return pl.pallas_call(
        body,
        out_shape=[jax.ShapeDtypeStruct(shape, dtype) for shape, dtype in outs],
        in_specs=[smem] * scalars + [vmem] * (len(args) - scalars - far) + [hbm] * far,
        out_specs=[vmem] * len(outs),
        scratch_shapes=scratch,
        compiler_params=pltpu.CompilerParams(vmem_limit_bytes=limit * MIB),
        cost_estimate=cost,
    )(*args)


def start_copies(pairs, sems):
    copies = [pltpu.make_async_copy(src, dst, sems.at[i]) for i, (src, dst) in enumerate(pairs)]
    for copy in copies:
        copy.start()
    return copies


def finish(copies):
    for copy in copies:
        copy.wait()


def pieces(source, target, start):
    size = target.shape[0] // PIECES
    return [
        (source.at[pl.ds(start + i * size, size), :], target.at[pl.ds(i * size, size), :])
        for i in range(PIECES)
    ]


def fetch_rows_kernel(start, after, source, out, token, sems):
    copies = start_copies(pieces(source, out, start), sems)
    token[...] = jnp.zeros(token.shape, F32)
    finish(copies)


def normalized(block, gain):
    values = f32(block)
    mean_square = jnp.mean(values * values, axis=-1, keepdims=True)
    return (values * lax.rsqrt(mean_square + EPS) * gain).astype(BF16)


def sigmoid_times(values):
    return values / (1.0 + jnp.exp(-values))


def stage_kernel(
    place,
    in_weight,
    cache,
    select,
    hidden,
    gain,
    ffn_gain,
    conv_weight,
    conv_bias,
    step_bias,
    skip_gain,
    step_gain,
    decay,
    experts,
    share,
    in_weight_out,
    cache_out,
    select_out,
    hidden_out,
    gain_out,
    ffn_gain_out,
    columns,
    step_gain_out,
    rates,
    weights,
    conv_weight_in,
    conv_bias_in,
    step_bias_in,
    skip_gain_in,
    step_gain_in,
    decay_in,
    experts_in,
    share_in,
    packed,
    sems,
):
    small = start_copies(
        (
            (conv_weight, conv_weight_in),
            (conv_bias, conv_bias_in),
            (step_bias, step_bias_in),
            (skip_gain, skip_gain_in),
            (step_gain, step_gain_in),
            (decay, decay_in),
            (experts, experts_in),
            (share, share_in),
        ),
        sems,
    )
    large = start_copies(
        (
            (in_weight, in_weight_out),
            (cache, cache_out),
            (select, select_out),
            (hidden, hidden_out),
            (gain, gain_out),
            (ffn_gain, ffn_gain_out),
        ),
        sems.at[pl.ds(len(small), 6)],
    )
    finish(small)
    taps, channels = conv_weight.shape
    packed[...] = jnp.zeros(packed.shape, F32)
    packed[:taps, :channels] = conv_weight_in[...]
    packed[taps : taps + 1, :channels] = conv_bias_in[...]
    packed[taps + 1 : taps + 2, :channels] = step_bias_in[...]
    packed[taps + 2 : taps + 3, :channels] = skip_gain_in[...]
    columns[...] = packed[...].T[:channels, :]
    rank = step_gain.shape[1]
    packed[:1, :rank] = step_gain_in[...]
    step_gain_out[...] = packed[...].T[:rank, :]
    topk, count = experts.shape
    packed[:topk, :count] = f32(experts_in[...])
    packed[topk : 2 * topk, :count] = share_in[...]
    turned = packed[:, :LANES].T[:count, :]
    lane = lax.broadcasted_iota(jnp.int32, (count, LANES), 1)
    first = lane < LANES // 2
    number = f32(jnp.where(first, lane, lane - LANES // 2))
    dense = jnp.zeros(lane.shape, F32)
    for k in range(topk):
        hit = number == turned[:, k : k + 1]
        dense = dense + jnp.where(hit, turned[:, topk + k : topk + k + 1], 0.0)
    upper = dense.astype(BF16)
    lower = (dense - f32(upper)).astype(BF16)
    weights[...] = jnp.where(first, f32(upper), f32(lower)).astype(BF16)
    rate = -jnp.exp(decay_in[...])
    for c in range(channels):
        rates[c] = jnp.broadcast_to(rate[:, c : c + 1], rates.shape[1:])
    finish(large)


def project_kernel(blocks, place, *refs):
    rows = refs[:blocks]
    gain, weight, cache, columns, select, out_weight, step_weight, states = refs[
        blocks : blocks + 8
    ]
    (
        conved_out,
        gate_out,
        keep,
        send,
        out_weight_out,
        step_weight_out,
        states_out,
        normed,
        selected,
        sems,
    ) = refs[blocks + 8 :]
    copies = start_copies(
        (
            (out_weight, out_weight_out),
            (step_weight, step_weight_out),
            (states, states_out),
        ),
        sems,
    )
    me = place[0]
    count = rows[0].shape[0]
    for j in range(blocks):
        start = pl.multiple_of((me ^ j) * count, count)
        normed[pl.ds(start, count), :] = normalized(rows[j][...], gain[...])
    dims = (((1,), (1,)), ((), ()))
    x_input = lax.dot_general(weight[0], normed[...], dims, preferred_element_type=F32)
    pre_conv = columns[:, 4:5] + columns[:, 3:4] * x_input
    for tap in range(3):
        pre_conv = pre_conv + columns[:, tap : tap + 1] * f32(cache[tap])
    conved = sigmoid_times(pre_conv)
    conved_out[...] = conved
    selected[...] = jnp.dot(select[...], conved.astype(BF16), preferred_element_type=F32)
    half = keep.shape[0]
    side = me & 1
    keep[...] = selected[pl.ds(pl.multiple_of(side * half, 16), half), :].astype(BF16)
    send[...] = selected[pl.ds(pl.multiple_of((1 - side) * half, 16), half), :].astype(BF16)
    z_gate = lax.dot_general(weight[1], normed[...], dims, preferred_element_type=F32)
    gate_out[...] = sigmoid_times(z_gate)
    finish(copies)


def state_kernel(
    blocks,
    place,
    own_half,
    other_half,
    step_gain,
    step_weight,
    columns,
    conved,
    gate,
    cache,
    rates,
    out_weight,
    new_state,
    keep,
    send,
    selected,
    step,
    driven,
    mixed,
    turned,
):
    me = place[0]
    side = me & 1
    half = own_half.shape[0]
    channels, states, rows = cache.shape
    rank = step_weight.shape[1]
    count = rows // blocks
    selected[pl.ds(pl.multiple_of(side * half, 16), half), :] = f32(own_half[...])
    selected[pl.ds(pl.multiple_of((1 - side) * half, 16), half), :] = f32(other_half[...])
    low = selected[:rank, :]
    mean_square = jnp.mean(low * low, axis=0, keepdims=True)
    step_low = (low * lax.rsqrt(mean_square + EPS) * step_gain[:, :1]).astype(BF16)
    raw = jnp.dot(step_weight[...], step_low, preferred_element_type=F32) + columns[:, 5:6]
    sizes = jnp.maximum(raw, 0.0) + jnp.log1p(jnp.exp(-jnp.abs(raw)))
    step[...] = sizes
    driven[...] = sizes * conved[...]
    in_coef = selected[rank : rank + states, :]
    out_coef = selected[rank + states :, :]

    def channel(c, carry):
        one = pl.ds(c, 1)
        state = jnp.exp(step[one, :] * rates[c]) * f32(cache[c]) + driven[one, :] * in_coef
        new_state[c] = state.astype(BF16)
        mixed[one, :] = jnp.sum(state * out_coef, axis=0, keepdims=True)
        return carry

    lax.fori_loop(0, channels, channel, 0, unroll=8)
    gated = (mixed[...] + columns[:, 6:7] * conved[...]) * gate[...]
    turned[...] = gated.T
    parts = []
    for side_of in range(2):
        for k in range(blocks // 2):
            start = pl.multiple_of((me ^ (2 * k + side_of)) * count, count)
            parts.append(turned[pl.ds(start, count), :].astype(BF16))
    left = jnp.concatenate(parts, axis=0)
    kept = keep.shape[0]
    width = out_weight.shape[1]
    piece = 512 if width % 512 == 0 else width
    for start in range(0, width, piece):
        span = slice(start, start + piece)
        partial = jnp.dot(left, out_weight[:, span], preferred_element_type=F32).astype(BF16)
        keep[:, span] = partial[:kept]
        send[:, span] = partial[kept:]


def split_kernel(keep, got, *outs):
    count = outs[0].shape[0]
    for k, out in enumerate(outs):
        span = slice(k * count, (k + 1) * count)
        out[...] = (f32(keep[span, :]) + f32(got[span, :])).astype(BF16)


def add_kernel(count, *refs):
    total = f32(refs[0][...])
    for ref in refs[1:count]:
        total = total + f32(ref[...])
    refs[-1][...] = total.astype(refs[-1].dtype)


def residual_kernel(mine, got, hidden, weights, token, out):
    width = hidden.shape[1]
    residual = f32(hidden[...]) + (f32(mine[...]) + f32(got[...]))
    out[:, :width] = residual.astype(BF16)
    out[:, width:] = weights[...]


def expert_kernel(blocks, group, place, *refs):
    rows = refs[:blocks]
    gain, *downs = refs[blocks : blocks + 4]
    gate_proj, up_proj = refs[blocks + 4 : blocks + 6]
    keep, send, normed, share, total, gates, ups, sems = refs[blocks + 6 :]
    count = rows[0].shape[0]
    width = gain.shape[1]
    size = gates.shape[2]
    steps = gate_proj.shape[1] // size

    def copies(i, slot):
        span = pl.ds(pl.multiple_of(i * size, size), size)
        return (
            pltpu.make_async_copy(gate_proj.at[:, span], gates.at[slot], sems.at[slot, 0]),
            pltpu.make_async_copy(up_proj.at[:, span], ups.at[slot], sems.at[slot, 1]),
        )

    def begin(i, slot):
        for copy in copies(i, slot):
            copy.start()

    for i in range(min(2, steps)):
        begin(i, i)
    expert = place[0] // group
    lane = lax.broadcasted_iota(jnp.int32, (count, LANES), 1)
    wanted = (lane == expert) | (lane == expert + LANES // 2)
    for j in range(blocks):
        span = slice(j * count, (j + 1) * count)
        normed[span, :] = normalized(rows[j][:, :width], gain[...])
        shares = jnp.where(wanted, f32(rows[j][:, width:]), 0.0)
        share[span, :] = jnp.broadcast_to(jnp.sum(shares, axis=1, keepdims=True), (count, LANES))

    def inner_of(gate_block, up_block):
        inputs = normed[...]
        gate_act = jnp.dot(inputs, gate_block, preferred_element_type=F32)
        up_act = jnp.dot(inputs, up_block, preferred_element_type=F32)
        return (sigmoid_times(gate_act) * up_act).astype(BF16)

    total[...] = jnp.zeros(total.shape, F32)
    group = 2 if all(down.shape[0] % (2 * size) == 0 for down in downs) else 1
    first = 0
    for down in downs:
        last = first + down.shape[0] // size

        def step(j, carry, down=down, first=first):
            parts = []
            for part in range(group):
                i = first + j * group + part
                slot = part if group == 2 else lax.rem(i, 2)
                finish(copies(i, slot))
                parts.append(inner_of(gates[slot], ups[slot]))

                @pl.when(i + 2 < steps)
                def _(i=i, slot=slot):
                    begin(i + 2, slot)

            inner = jnp.concatenate(parts, axis=1)
            span = pl.ds(pl.multiple_of(j * group * size, size), group * size)
            total[...] += jnp.dot(inner, down[span, :], preferred_element_type=F32)
            return carry

        lax.fori_loop(0, (last - first) // group, step, 0)
        first = last
    weighted = (total[...] * share[:, :1]).astype(BF16)
    kept = keep.shape[0]
    keep[...] = weighted[:kept]
    send[...] = weighted[kept:]


def columns_kernel(place, *refs):
    outs = refs[-place_count(refs) :]
    ins = refs[: -len(outs)]
    size = outs[0].shape[1]
    me = place[1]
    for k, out in enumerate(outs):
        span = pl.ds(pl.multiple_of((me ^ k) * size, size), size)
        total = f32(ins[0][:, span])
        for ref in ins[1:]:
            total = total + f32(ref[:, span])
        out[...] = total.astype(BF16)


def place_count(refs):
    return refs[0].shape[1] // refs[-1].shape[1]


def final_kernel(place, residual, *refs):
    out = refs[-1]
    size = out.shape[1]
    span = pl.ds(pl.multiple_of(place[1] * size, size), size)
    total = f32(refs[0][...])
    for ref in refs[1:-1]:
        total = total + f32(ref[...])
    out[...] = (f32(residual[:, span]) + total).astype(BF16)


def on_device(
    hidden,
    conv_cache,
    ssm_cache,
    mixer_gain,
    in_weight,
    conv_weight,
    conv_bias,
    select_weight,
    step_gain,
    step_weight,
    step_bias,
    decay_log,
    skip_gain,
    out_weight,
    ffn_gain,
    gate_proj,
    up_proj,
    down_proj,
    route_experts,
    route_share,
):
    narrow_count = lax.axis_size("narrow")
    wide_count = lax.axis_size("wide")
    chips = wide_count // 2
    count, width = hidden.shape
    rows = count * wide_count
    channels, states = decay_log.shape
    chosen = select_weight.shape[1]
    hidden_units = gate_proj.shape[1]

    def swap(values):
        return lax.ppermute(values, "wide", [(i, i ^ 1) for i in range(wide_count)])

    def to_chip(values, k):
        return lax.ppermute(values, "wide", [(i, i ^ (2 * k)) for i in range(wide_count)])

    def to_narrow(values, k):
        return lax.ppermute(values, "narrow", [(i, i ^ k) for i in range(narrow_count)])

    def fetch_rows(start, size, after):
        return kernel_call(
            functools.partial(fetch_rows_kernel, start),
            [((size, width), BF16), ((8, LANES), F32)],
            (after, down_proj),
            scalars=0,
            far=1,
            scratch=[pltpu.SemaphoreType.DMA((PIECES,))],
            cost=pl.CostEstimate(flops=0, bytes_accessed=4 * size * width, transcendentals=0),
        )

    def plane_gather(block, near):
        same = [near, *[to_chip(block, k) for k in range(1, chips)]]
        other = [swap(item) for item in same]
        return same, other

    def plane_scatter(keep, got):
        return kernel_call(split_kernel, [((count, width), BF16)] * chips, (keep, got), scalars=0)

    def to_chips(parts):
        return [to_chip(parts[k], k) for k in range(1, chips)]

    def add(*items, token=None):
        args = items if token is None else (*items, token)
        body = functools.partial(add_kernel, len(items))
        return kernel_call(body, [(items[0].shape, BF16)], args, scalars=0)[0]

    place = jnp.stack([lax.axis_index("wide"), lax.axis_index("narrow")]).astype(jnp.int32)
    block = next(size for size in (256, 128, hidden_units) if hidden_units % size == 0)
    steps = hidden_units // block
    third = max(1, steps // 3) * block
    rank = step_weight.shape[1]
    topk = route_experts.shape[1]
    padded = max(LANES, channels, rank)
    (
        in_weight_near,
        conv_cache_near,
        select_near,
        hidden_near,
        mixer_gain_near,
        ffn_gain_near,
        columns,
        step_gain_column,
        rates,
        weights,
    ) = kernel_call(
        stage_kernel,
        [
            (in_weight.shape, BF16),
            (conv_cache.shape, BF16),
            ((chosen, channels), BF16),
            (hidden.shape, BF16),
            ((1, width), F32),
            ((1, width), F32),
            ((channels, LANES), F32),
            ((rank, LANES), F32),
            ((channels, states, rows), F32),
            ((count, LANES), BF16),
        ],
        (
            place,
            in_weight,
            conv_cache,
            select_weight.T,
            hidden,
            mixer_gain[None, :],
            ffn_gain[None, :],
            conv_weight,
            conv_bias[None, :],
            step_bias[None, :],
            skip_gain[None, :],
            step_gain[None, :],
            decay_log.T,
            route_experts.T,
            route_share.T,
        ),
        far=14,
        scratch=[
            pltpu.VMEM(conv_weight.shape, F32),
            pltpu.VMEM((1, channels), F32),
            pltpu.VMEM((1, channels), F32),
            pltpu.VMEM((1, channels), F32),
            pltpu.VMEM((1, rank), F32),
            pltpu.VMEM((states, channels), F32),
            pltpu.VMEM((topk, count), jnp.int32),
            pltpu.VMEM((topk, count), F32),
            pltpu.VMEM((LANES, padded), F32),
            pltpu.SemaphoreType.DMA((14,)),
        ],
        cost=pl.CostEstimate(
            flops=0,
            bytes_accessed=4 * in_weight.size,
            transcendentals=decay_log.size,
        ),
    )

    same, other = plane_gather(hidden, hidden_near)
    interleaved = [item for pair in zip(same, other) for item in pair]
    half = chosen // 2
    conved, gate, keep, send, out_weight_near, step_weight_near, states_near = kernel_call(
        functools.partial(project_kernel, wide_count),
        [
            ((channels, rows), F32),
            ((channels, rows), F32),
            ((half, rows), BF16),
            ((half, rows), BF16),
            (out_weight.shape, BF16),
            (step_weight.shape, BF16),
            (ssm_cache.shape, BF16),
        ],
        (
            place,
            *interleaved,
            mixer_gain_near,
            in_weight_near,
            conv_cache_near,
            columns,
            select_near,
            out_weight,
            step_weight,
            ssm_cache,
        ),
        far=3,
        scratch=[
            pltpu.VMEM((rows, width), BF16),
            pltpu.VMEM((chosen, rows), F32),
            pltpu.SemaphoreType.DMA((3,)),
        ],
    )
    part = add(keep, swap(send))
    part = add(part, *[to_chip(part, k) for k in range(1, chips)])
    part = add(part, *[to_narrow(part, k) for k in range(1, narrow_count)])
    new_state, keep, send = kernel_call(
        functools.partial(state_kernel, wide_count),
        [
            (ssm_cache.shape, BF16),
            ((rows // 2, width), BF16),
            ((rows // 2, width), BF16),
        ],
        (
            place,
            part,
            swap(part),
            step_gain_column,
            step_weight_near,
            columns,
            conved,
            gate,
            states_near,
            rates,
            out_weight_near,
        ),
        scratch=[
            pltpu.VMEM((chosen, rows), F32),
            pltpu.VMEM((channels, rows), F32),
            pltpu.VMEM((channels, rows), F32),
            pltpu.VMEM((channels, rows), F32),
            pltpu.VMEM((rows, channels), F32),
        ],
    )
    parts = plane_scatter(keep, swap(send))
    down_first, token = fetch_rows(0, third, parts[0])
    mine = add(parts[0], *to_chips(parts), token=token)
    down_second, token = fetch_rows(third, third, mine)
    step = 1
    while 2 * step < narrow_count:
        mine = add(mine, to_narrow(mine, step), token=token)
        step *= 2
    down_third, token = fetch_rows(2 * third, hidden_units - 2 * third, mine)
    (residual,) = kernel_call(
        residual_kernel,
        [((count, width + LANES), BF16)],
        (mine, to_narrow(mine, step), hidden_near, weights, token),
        scalars=0,
    )
    same, other = plane_gather(residual, residual)
    keep, send = kernel_call(
        functools.partial(expert_kernel, wide_count, wide_count // EXPERTS),
        [((rows // 2, width), BF16)] * 2,
        (
            place,
            *same,
            *other,
            ffn_gain_near,
            down_first,
            down_second,
            down_third,
            gate_proj,
            up_proj,
        ),
        far=2,
        scratch=[
            pltpu.VMEM((rows, width), BF16),
            pltpu.VMEM((rows, LANES), F32),
            pltpu.VMEM((rows, width), F32),
            pltpu.VMEM((2, width, block), BF16),
            pltpu.VMEM((2, width, block), BF16),
            pltpu.SemaphoreType.DMA((2, 2)),
        ],
        limit=20,
    )
    parts = plane_scatter(keep, swap(send))
    parts = [parts[0], *to_chips(parts)]
    col_share = width // narrow_count
    shares = kernel_call(
        columns_kernel, [((count, col_share), BF16)] * narrow_count, (place, *parts)
    )
    (layer_out,) = kernel_call(
        final_kernel,
        [((count, col_share), BF16)],
        (
            place,
            residual,
            shares[0],
            *[to_narrow(shares[k], k) for k in range(1, narrow_count)],
        ),
    )
    return (layer_out, new_state)


def solution(mesh):
    placed = (
        P("wide", None),
        P(None, ("wide", "narrow"), None),
        P(("wide", "narrow"), None, None),
        P(),
        P(None, ("wide", "narrow"), None),
        P(None, ("wide", "narrow")),
        P(("wide", "narrow")),
        P(("wide", "narrow"), None),
        P(),
        P(("wide", "narrow"), None),
        P(("wide", "narrow")),
        P(("wide", "narrow"), None),
        P(("wide", "narrow")),
        P(("wide", "narrow"), None),
        P(),
        P(None, ("wide", "narrow")),
        P(None, ("wide", "narrow")),
        P(("wide", "narrow"), None),
        P("wide", None),
        P("wide", None),
    )
    return jax.shard_map(
        on_device,
        mesh=mesh,
        in_specs=placed,
        out_specs=(P("wide", "narrow"), P(("wide", "narrow"), None, None)),
        check_vma=False,
    )
```

```python
import functools

import jax
import jax.numpy as jnp
from jax import lax
from jax.experimental import pallas as pl
from jax.experimental.pallas import tpu as pltpu
from jax.sharding import PartitionSpec as P

EXPERTS = 8
EPS = 1e-06
MIB = 1 << 20
LANES = 128
PIECES = 2
F32 = jnp.float32
BF16 = jnp.bfloat16


def f32(values):
    return values.astype(F32)


def kernel_call(body, outs, args, far=0, scratch=(), limit=16, cost=None, pinned=0):
    vmem = pl.BlockSpec(memory_space=pltpu.VMEM)
    hbm = pl.BlockSpec(memory_space=pltpu.HBM)
    near = len(args) - far
    stay = [pltpu.with_memory_space_constraint(item, pltpu.HBM) for item in args[near:]]
    args = (*args[:near], *stay)
    return pl.pallas_call(
        body,
        out_shape=[
            pltpu.VMEM(*out) if i < pinned else jax.ShapeDtypeStruct(*out)
            for i, out in enumerate(outs)
        ],
        in_specs=[vmem] * near + [hbm] * far,
        out_specs=[vmem] * len(outs),
        scratch_shapes=scratch,
        compiler_params=pltpu.CompilerParams(vmem_limit_bytes=limit * MIB),
        cost_estimate=cost,
    )(*args)


def start_copies(pairs, sems):
    copies = [pltpu.make_async_copy(src, dst, sems.at[i]) for i, (src, dst) in enumerate(pairs)]
    for copy in copies:
        copy.start()
    return copies


def finish(copies):
    for copy in copies:
        copy.wait()


def fetch_rows_kernel(start, after, source, *refs):
    *outs, token, sems = refs
    size = outs[0].shape[0] // PIECES
    pairs = []
    for i, out in enumerate(outs):
        for j in range(PIECES):
            first = start + (i * PIECES + j) * size
            pairs.append((source.at[pl.ds(first, size), :], out.at[pl.ds(j * size, size), :]))
    copies = start_copies(pairs, sems)
    token[...] = jnp.zeros(token.shape, F32)
    finish(copies)


def fetch_kernel(after, first, second, third, first_out, second_out, third_out, token, sems):
    copies = start_copies(((first, first_out), (second, second_out), (third, third_out)), sems)
    token[...] = jnp.zeros(token.shape, F32)
    finish(copies)


def fetch_columns_kernel(block, first, second, first_out, second_out, block_out, sems):
    size = first_out.shape[1]
    copies = start_copies(
        ((first.at[:, pl.ds(0, size)], first_out), (second.at[:, pl.ds(0, size)], second_out)),
        sems,
    )
    block_out[...] = block[...]
    finish(copies)


def normalized(block, gain):
    values = f32(block)
    mean_square = jnp.mean(values * values, axis=-1, keepdims=True)
    return (values * lax.rsqrt(mean_square + EPS) * gain).astype(BF16)


def sigmoid_times(values):
    return values / (1.0 + jnp.exp(-values))


def stage_kernel(
    in_weight,
    cache,
    select,
    hidden,
    gain,
    ffn_gain,
    conv_weight,
    conv_bias,
    step_bias,
    skip_gain,
    step_gain,
    decay,
    experts,
    share,
    in_weight_out,
    cache_out,
    select_out,
    hidden_out,
    gain_out,
    ffn_gain_out,
    columns,
    step_gain_out,
    rates,
    weights,
    conv_weight_in,
    conv_bias_in,
    step_bias_in,
    skip_gain_in,
    step_gain_in,
    decay_in,
    experts_in,
    share_in,
    packed,
    sems,
):
    small = start_copies(
        (
            (conv_weight, conv_weight_in),
            (conv_bias, conv_bias_in),
            (step_bias, step_bias_in),
            (skip_gain, skip_gain_in),
            (step_gain, step_gain_in),
            (decay, decay_in),
            (experts, experts_in),
            (share, share_in),
        ),
        sems,
    )
    large = start_copies(
        (
            (in_weight, in_weight_out),
            (cache, cache_out),
            (select, select_out),
            (hidden, hidden_out),
            (gain, gain_out),
            (ffn_gain, ffn_gain_out),
        ),
        sems.at[pl.ds(len(small), 6)],
    )
    finish(small)
    taps, channels = conv_weight.shape
    packed[...] = jnp.zeros(packed.shape, F32)
    packed[:taps, :channels] = conv_weight_in[...]
    packed[taps : taps + 1, :channels] = conv_bias_in[...]
    packed[taps + 1 : taps + 2, :channels] = step_bias_in[...]
    packed[taps + 2 : taps + 3, :channels] = skip_gain_in[...]
    columns[...] = packed[...].T[:channels, :]
    rank = step_gain.shape[1]
    packed[:1, :rank] = step_gain_in[...]
    step_gain_out[...] = packed[...].T[:rank, :]
    topk, count = experts.shape
    packed[:topk, :count] = f32(experts_in[...])
    packed[topk : 2 * topk, :count] = share_in[...]
    turned = packed[:, :LANES].T[:count, :]
    lane = lax.broadcasted_iota(jnp.int32, (count, LANES), 1)
    first = lane < LANES // 2
    number = f32(jnp.where(first, lane, lane - LANES // 2))
    dense = jnp.zeros(lane.shape, F32)
    for k in range(topk):
        hit = number == turned[:, k : k + 1]
        dense = dense + jnp.where(hit, turned[:, topk + k : topk + k + 1], 0.0)
    upper = dense.astype(BF16)
    lower = (dense - f32(upper)).astype(BF16)
    weights[...] = jnp.where(first, f32(upper), f32(lower)).astype(BF16)
    rate = -jnp.exp(decay_in[...])
    for c in range(channels):
        rates[c] = jnp.broadcast_to(rate[:, c : c + 1], rates.shape[1:])
    finish(large)


def project_kernel(blocks, *refs):
    rows = refs[:blocks]
    gain, weight, cache, columns, select = refs[blocks : blocks + 5]
    conved_out, gate_out, keep, send, normed, selected = refs[blocks + 5 :]
    me = lax.axis_index("wide")
    count = rows[0].shape[0]
    for j in range(blocks):
        start = pl.multiple_of((me ^ j) * count, count)
        normed[pl.ds(start, count), :] = normalized(rows[j][...], gain[...])
    dims = (((1,), (1,)), ((), ()))
    x_input = lax.dot_general(weight[0], normed[...], dims, preferred_element_type=F32)
    pre_conv = columns[:, 4:5] + columns[:, 3:4] * x_input
    for tap in range(3):
        pre_conv = pre_conv + columns[:, tap : tap + 1] * f32(cache[tap])
    conved = sigmoid_times(pre_conv)
    conved_out[...] = conved
    selected[...] = jnp.dot(select[...], conved.astype(BF16), preferred_element_type=F32)
    half = keep.shape[0]
    side = me & 1
    keep[...] = selected[pl.ds(pl.multiple_of(side * half, 16), half), :].astype(BF16)
    send[...] = selected[pl.ds(pl.multiple_of((1 - side) * half, 16), half), :].astype(BF16)
    z_gate = lax.dot_general(weight[1], normed[...], dims, preferred_element_type=F32)
    gate_out[...] = sigmoid_times(z_gate)


def state_kernel(
    blocks,
    own_half,
    other_half,
    step_gain,
    step_weight,
    columns,
    conved,
    gate,
    cache,
    rates,
    out_weight,
    new_state,
    keep,
    send,
    selected,
    step,
    driven,
    mixed,
    turned,
):
    me = lax.axis_index("wide")
    side = me & 1
    half = own_half.shape[0]
    channels, states, rows = cache.shape
    rank = step_weight.shape[1]
    count = rows // blocks
    selected[pl.ds(pl.multiple_of(side * half, 16), half), :] = f32(own_half[...])
    selected[pl.ds(pl.multiple_of((1 - side) * half, 16), half), :] = f32(other_half[...])
    low = selected[:rank, :]
    mean_square = jnp.mean(low * low, axis=0, keepdims=True)
    step_low = (low * lax.rsqrt(mean_square + EPS) * step_gain[:, :1]).astype(BF16)
    raw = jnp.dot(step_weight[...], step_low, preferred_element_type=F32) + columns[:, 5:6]
    sizes = jnp.maximum(raw, 0.0) + jnp.log1p(jnp.exp(-jnp.abs(raw)))
    step[...] = sizes
    driven[...] = sizes * conved[...]
    in_coef = selected[rank : rank + states, :]
    out_coef = selected[rank + states :, :]

    def channel(c, carry):
        one = pl.ds(c, 1)
        state = jnp.exp(step[one, :] * rates[c]) * f32(cache[c]) + driven[one, :] * in_coef
        new_state[c] = state.astype(BF16)
        mixed[one, :] = jnp.sum(state * out_coef, axis=0, keepdims=True)
        return carry

    lax.fori_loop(0, channels, channel, 0, unroll=8)
    gated = (mixed[...] + columns[:, 6:7] * conved[...]) * gate[...]
    turned[...] = gated.T
    parts = []
    for side_of in range(2):
        for k in range(blocks // 2):
            start = pl.multiple_of((me ^ (2 * k + side_of)) * count, count)
            parts.append(turned[pl.ds(start, count), :].astype(BF16))
    left = jnp.concatenate(parts, axis=0)
    kept = keep.shape[0]
    width = out_weight.shape[1]
    piece = 512 if width % 512 == 0 else width
    for start in range(0, width, piece):
        span = slice(start, start + piece)
        partial = jnp.dot(left, out_weight[:, span], preferred_element_type=F32).astype(BF16)
        keep[:, span] = partial[:kept]
        send[:, span] = partial[kept:]


def split_kernel(keep, got, *outs):
    count = outs[0].shape[0]
    for k, out in enumerate(outs):
        span = slice(k * count, (k + 1) * count)
        out[...] = (f32(keep[span, :]) + f32(got[span, :])).astype(BF16)


def add_kernel(count, *refs):
    total = f32(refs[0][...])
    for ref in refs[1:count]:
        total = total + f32(ref[...])
    refs[-1][...] = total.astype(refs[-1].dtype)


def residual_kernel(mine, got, hidden, weights, token, out):
    width = hidden.shape[1]
    residual = f32(hidden[...]) + (f32(mine[...]) + f32(got[...]))
    out[:, :width] = residual.astype(BF16)
    out[:, width:] = weights[...]


def expert_kernel(blocks, steps, group, *refs):
    rows = refs[:blocks]
    gain, *downs = refs[blocks : blocks + 1 + steps]
    gate_first, up_first, gate_proj, up_proj = refs[blocks + 1 + steps : blocks + 5 + steps]
    keep, send, normed, share, total, gates, ups, sems = refs[blocks + 5 + steps :]
    count = rows[0].shape[0]
    width = gain.shape[1]
    size = gates.shape[2]

    def copies(i, slot):
        span = pl.ds(i * size, size)
        return (
            pltpu.make_async_copy(gate_proj.at[:, span], gates.at[slot], sems.at[slot, 0]),
            pltpu.make_async_copy(up_proj.at[:, span], ups.at[slot], sems.at[slot, 1]),
        )

    def begin(i, slot):
        for copy in copies(i, slot):
            copy.start()

    near = gate_first.shape[1]
    rest = size - near
    ahead = []
    if rest:
        span = pl.ds(near, rest)
        ahead = start_copies(
            (
                (gate_proj.at[:, span], gates.at[0, :, pl.ds(0, rest)]),
                (up_proj.at[:, span], ups.at[0, :, pl.ds(0, rest)]),
            ),
            sems.at[0],
        )
    for i in range(1, min(2 if rest else 3, steps)):
        begin(i, i % 2)
    expert = lax.axis_index("wide") // group
    lane = lax.broadcasted_iota(jnp.int32, (count, LANES), 1)
    wanted = (lane == expert) | (lane == expert + LANES // 2)
    for j in range(blocks):
        span = slice(j * count, (j + 1) * count)
        normed[span, :] = normalized(rows[j][:, :width], gain[...])
        shares = jnp.where(wanted, f32(rows[j][:, width:]), 0.0)
        share[span, :] = jnp.broadcast_to(jnp.sum(shares, axis=1, keepdims=True), (count, LANES))

    def inner_of(gate_block, up_block):
        inputs = normed[...]
        gate_act = jnp.dot(inputs, gate_block, preferred_element_type=F32)
        up_act = jnp.dot(inputs, up_block, preferred_element_type=F32)
        return (sigmoid_times(gate_act) * up_act).astype(BF16)

    inner = inner_of(gate_first[...], up_first[...])
    if rest:
        finish(ahead)
        more = inner_of(gates[0, :, :rest], ups[0, :, :rest])
        if steps > 2:
            begin(2, 0)
        inner = jnp.concatenate([inner, more], axis=1)
    total[...] = jnp.dot(inner, downs[0][...], preferred_element_type=F32)
    for i in range(1, steps):
        slot = i % 2
        finish(copies(i, slot))
        inner = inner_of(gates[slot], ups[slot])
        if i + 2 < steps:
            begin(i + 2, slot)
        total[...] += jnp.dot(inner, downs[i][...], preferred_element_type=F32)
    weighted = (total[...] * share[:, :1]).astype(BF16)
    kept = keep.shape[0]
    keep[...] = weighted[:kept]
    send[...] = weighted[kept:]


def columns_kernel(narrow_count, *refs):
    ins, outs = refs[:-narrow_count], refs[-narrow_count:]
    size = outs[0].shape[1]
    for me in range(narrow_count):

        @pl.when(lax.axis_index("narrow") == me)
        def _(me=me):
            for k, out in enumerate(outs):
                first = (me ^ k) * size
                span = slice(first, first + size)
                total = f32(ins[0][:, span])
                for ref in ins[1:]:
                    total = total + f32(ref[:, span])
                out[...] = total.astype(BF16)


def final_kernel(narrow_count, residual, *refs):
    *ins, out = refs
    size = out.shape[1]
    for me in range(narrow_count):

        @pl.when(lax.axis_index("narrow") == me)
        def _(me=me):
            total = f32(ins[0][...])
            for ref in ins[1:]:
                total = total + f32(ref[...])
            out[...] = (f32(residual[:, me * size : (me + 1) * size]) + total).astype(BF16)


def on_device(
    hidden,
    conv_cache,
    ssm_cache,
    mixer_gain,
    in_weight,
    conv_weight,
    conv_bias,
    select_weight,
    step_gain,
    step_weight,
    step_bias,
    decay_log,
    skip_gain,
    out_weight,
    ffn_gain,
    gate_proj,
    up_proj,
    down_proj,
    route_experts,
    route_share,
):
    narrow_count = lax.axis_size("narrow")
    wide_count = lax.axis_size("wide")
    chips = wide_count // 2
    count, width = hidden.shape
    rows = count * wide_count
    channels, states = decay_log.shape
    chosen = select_weight.shape[1]
    hidden_units = gate_proj.shape[1]

    def swap(values):
        return lax.ppermute(values, "wide", [(i, i ^ 1) for i in range(wide_count)])

    def to_chip(values, k):
        return lax.ppermute(values, "wide", [(i, i ^ (2 * k)) for i in range(wide_count)])

    def to_narrow(values, k):
        return lax.ppermute(values, "narrow", [(i, i ^ k) for i in range(narrow_count)])

    def fetch_rows(start, number, after):
        *blocks, token = kernel_call(
            functools.partial(fetch_rows_kernel, start * block),
            [((block, width), BF16)] * number + [((8, LANES), F32)],
            (after, down_proj),
                far=1,
            scratch=[pltpu.SemaphoreType.DMA((number * PIECES,))],
            cost=pl.CostEstimate(
                flops=0, bytes_accessed=4 * number * block * width, transcendentals=0
            ),
        )
        return blocks, token

    def fetch_columns(size, after):
        return kernel_call(
            fetch_columns_kernel,
            [((width, size), BF16), ((width, size), BF16), (after.shape, BF16)],
            (after, gate_proj, up_proj),
                far=2,
            scratch=[pltpu.SemaphoreType.DMA((2,))],
            cost=pl.CostEstimate(flops=0, bytes_accessed=8 * size * width, transcendentals=0),
            pinned=2,
        )

    def plane_gather(block, near):
        same = [near, *[to_chip(block, k) for k in range(1, chips)]]
        other = [swap(item) for item in same]
        return same, other

    def plane_scatter(keep, got):
        return kernel_call(split_kernel, [((count, width), BF16)] * chips, (keep, got))

    def to_chips(parts):
        return [to_chip(parts[k], k) for k in range(1, chips)]

    def add(*items, token=None):
        args = items if token is None else (*items, token)
        body = functools.partial(add_kernel, len(items))
        return kernel_call(body, [(items[0].shape, BF16)], args)[0]

    block = next(size for size in (512, 256, 128, hidden_units) if hidden_units % size == 0)
    steps = hidden_units // block
    third = max(1, steps // 3)
    near = block // 2 if block % (2 * LANES) == 0 else block
    rank = step_weight.shape[1]
    topk = route_experts.shape[1]
    padded = max(LANES, channels, rank)
    (
        in_weight_near,
        conv_cache_near,
        select_near,
        hidden_near,
        mixer_gain_near,
        ffn_gain_near,
        columns,
        step_gain_column,
        rates,
        weights,
    ) = kernel_call(
        stage_kernel,
        [
            (in_weight.shape, BF16),
            (conv_cache.shape, BF16),
            ((chosen, channels), BF16),
            (hidden.shape, BF16),
            ((1, width), F32),
            ((1, width), F32),
            ((channels, LANES), F32),
            ((rank, LANES), F32),
            ((channels, states, rows), F32),
            ((count, LANES), BF16),
        ],
        (
            in_weight,
            conv_cache,
            select_weight.T,
            hidden,
            mixer_gain[None, :],
            ffn_gain[None, :],
            conv_weight,
            conv_bias[None, :],
            step_bias[None, :],
            skip_gain[None, :],
            step_gain[None, :],
            decay_log.T,
            route_experts.T,
            route_share.T,
        ),
        far=14,
        scratch=[
            pltpu.VMEM(conv_weight.shape, F32),
            pltpu.VMEM((1, channels), F32),
            pltpu.VMEM((1, channels), F32),
            pltpu.VMEM((1, channels), F32),
            pltpu.VMEM((1, rank), F32),
            pltpu.VMEM((states, channels), F32),
            pltpu.VMEM((topk, count), jnp.int32),
            pltpu.VMEM((topk, count), F32),
            pltpu.VMEM((LANES, padded), F32),
            pltpu.SemaphoreType.DMA((14,)),
        ],
        cost=pl.CostEstimate(
            flops=0,
            bytes_accessed=4 * in_weight.size,
            transcendentals=decay_log.size,
        ),
    )

    same, other = plane_gather(hidden, hidden_near)
    interleaved = [item for pair in zip(same, other) for item in pair]
    half = chosen // 2
    conved, gate, keep, send = kernel_call(
        functools.partial(project_kernel, wide_count),
        [
            ((channels, rows), F32),
            ((channels, rows), F32),
            ((half, rows), BF16),
            ((half, rows), BF16),
        ],
        (
            *interleaved,
            mixer_gain_near,
            in_weight_near,
            conv_cache_near,
            columns,
            select_near,
        ),
        scratch=[
            pltpu.VMEM((rows, width), BF16),
            pltpu.VMEM((chosen, rows), F32),
        ],
    )
    part = add(keep, swap(send))
    out_weight_near, step_weight_near, states_near, token = kernel_call(
        fetch_kernel,
        [
            (out_weight.shape, BF16),
            (step_weight.shape, BF16),
            (ssm_cache.shape, BF16),
            ((8, LANES), F32),
        ],
        (part, out_weight, step_weight, ssm_cache),
        far=3,
        scratch=[pltpu.SemaphoreType.DMA((3,))],
        cost=pl.CostEstimate(
            flops=0, bytes_accessed=4 * (out_weight.size + ssm_cache.size), transcendentals=0
        ),
    )
    part = add(part, *[to_chip(part, k) for k in range(1, chips)], token=token)
    part = add(part, *[to_narrow(part, k) for k in range(1, narrow_count)])
    new_state, keep, send = kernel_call(
        functools.partial(state_kernel, wide_count),
        [
            (ssm_cache.shape, BF16),
            ((rows // 2, width), BF16),
            ((rows // 2, width), BF16),
        ],
        (
            part,
            swap(part),
            step_gain_column,
            step_weight_near,
            columns,
            conved,
            gate,
            states_near,
            rates,
            out_weight_near,
        ),
        scratch=[
            pltpu.VMEM((chosen, rows), F32),
            pltpu.VMEM((channels, rows), F32),
            pltpu.VMEM((channels, rows), F32),
            pltpu.VMEM((channels, rows), F32),
            pltpu.VMEM((rows, channels), F32),
        ],
    )
    parts = plane_scatter(keep, swap(send))
    down_first, token = fetch_rows(0, third, parts[0])
    mine = add(parts[0], *to_chips(parts), token=token)
    down_second, token = fetch_rows(third, third, mine)
    step = 1
    while 2 * step < narrow_count:
        mine = add(mine, to_narrow(mine, step), token=token)
        step *= 2
    down_third, token = fetch_rows(2 * third, steps - 2 * third, mine)
    (residual,) = kernel_call(
        residual_kernel,
        [((count, width + LANES), BF16)],
        (mine, to_narrow(mine, step), hidden_near, weights, token),
    )
    gate_first, up_first, residual_near = fetch_columns(near, residual)
    same, other = plane_gather(residual, residual_near)
    keep, send = kernel_call(
        functools.partial(expert_kernel, wide_count, steps, wide_count // EXPERTS),
        [((rows // 2, width), BF16)] * 2,
        (
            *same,
            *other,
            ffn_gain_near,
            *down_first,
            *down_second,
            *down_third,
            gate_first,
            up_first,
            gate_proj,
            up_proj,
        ),
        far=2,
        scratch=[
            pltpu.VMEM((rows, width), BF16),
            pltpu.VMEM((rows, LANES), F32),
            pltpu.VMEM((rows, width), F32),
            pltpu.VMEM((2, width, block), BF16),
            pltpu.VMEM((2, width, block), BF16),
            pltpu.SemaphoreType.DMA((2, 2)),
        ],
        limit=22,
    )
    parts = plane_scatter(keep, swap(send))
    parts = [parts[0], *to_chips(parts)]
    col_share = width // narrow_count
    shares = kernel_call(
        functools.partial(columns_kernel, narrow_count),
        [((count, col_share), BF16)] * narrow_count, parts
    )
    (layer_out,) = kernel_call(
        functools.partial(final_kernel, narrow_count),
        [((count, col_share), BF16)],
        (
            residual,
            shares[0],
            *[to_narrow(shares[k], k) for k in range(1, narrow_count)],
        ),
    )
    return (layer_out, new_state)


def solution(mesh):
    placed = (
        P("wide", None),
        P(None, ("wide", "narrow"), None),
        P(("wide", "narrow"), None, None),
        P(),
        P(None, ("wide", "narrow"), None),
        P(None, ("wide", "narrow")),
        P(("wide", "narrow")),
        P(("wide", "narrow"), None),
        P(),
        P(("wide", "narrow"), None),
        P(("wide", "narrow")),
        P(("wide", "narrow"), None),
        P(("wide", "narrow")),
        P(("wide", "narrow"), None),
        P(),
        P(None, ("wide", "narrow")),
        P(None, ("wide", "narrow")),
        P(("wide", "narrow"), None),
        P("wide", None),
        P("wide", None),
    )
    return jax.shard_map(
        on_device,
        mesh=mesh,
        in_specs=placed,
        out_specs=(P("wide", "narrow"), P(("wide", "narrow"), None, None)),
        check_vma=False,
    )
```

```python
import functools

import jax
import jax.numpy as jnp
from jax import lax
from jax.experimental import pallas as pl
from jax.experimental.pallas import tpu as pltpu
from jax.sharding import PartitionSpec as P

EXPERTS = 8
EPS = 1e-06
MIB = 1 << 20
LANES = 128
PIECES = 2
F32 = jnp.float32
BF16 = jnp.bfloat16


def f32(values):
    return values.astype(F32)


def kernel_call(body, outs, args, far=0, scratch=(), limit=2, cost=None, far_outs=()):
    vmem = pl.BlockSpec(memory_space=pltpu.VMEM)
    hbm = pl.BlockSpec(memory_space=pltpu.HBM)
    near = len(args) - far
    stay = [pltpu.with_memory_space_constraint(item, pltpu.HBM) for item in args[near:]]
    args = (*args[:near], *stay)
    return pl.pallas_call(
        body,
        out_shape=[jax.ShapeDtypeStruct(*out) for out in outs],
        in_specs=[vmem] * near + [hbm] * far,
        out_specs=[hbm if i in far_outs else vmem for i in range(len(outs))],
        scratch_shapes=scratch,
        compiler_params=pltpu.CompilerParams(vmem_limit_bytes=limit * MIB),
        cost_estimate=cost,
    )(*args)


def start_copies(pairs, sems):
    copies = [pltpu.make_async_copy(src, dst, sems.at[i]) for i, (src, dst) in enumerate(pairs)]
    for copy in copies:
        copy.start()
    return copies


def finish(copies):
    for copy in copies:
        copy.wait()


def fetch_rows_kernel(start, stores, after, *refs):
    stored, (source, *outs), (token, sems) = refs[:stores], refs[stores:-2], refs[-2:]
    stored_out, outs = outs[len(outs) - stores :], outs[: len(outs) - stores]
    size = outs[0].shape[0] // PIECES
    pairs = list(zip(stored, stored_out))
    for i, out in enumerate(outs):
        for j in range(PIECES):
            first = start + (i * PIECES + j) * size
            pairs.append((source.at[pl.ds(first, size), :], out.at[pl.ds(j * size, size), :]))
    copies = start_copies(pairs, sems)
    token[...] = jnp.zeros(token.shape, F32)
    finish(copies)


def fetch_kernel(after, first, second, third, first_out, second_out, third_out, token, sems):
    copies = start_copies(((first, first_out), (second, second_out), (third, third_out)), sems)
    token[...] = jnp.zeros(token.shape, F32)
    finish(copies)


def fetch_columns_kernel(starts, block, first, second, *refs):
    *outs, block_out, sems = refs
    size = outs[0].shape[1] // 2
    pairs = []
    for start, out in zip(starts, outs, strict=True):
        span = pl.ds(start, size)
        pairs.append((first.at[:, span], out.at[:, pl.ds(0, size)]))
        pairs.append((second.at[:, span], out.at[:, pl.ds(size, size)]))
    copies = start_copies(pairs, sems)
    block_out[...] = block[...]
    finish(copies)


def normalized(block, gain):
    values = f32(block)
    mean_square = jnp.mean(values * values, axis=-1, keepdims=True)
    return (values * lax.rsqrt(mean_square + EPS) * gain).astype(BF16)


def sigmoid_times(values):
    return values / (1.0 + jnp.exp(-values))


def stage_kernel(
    in_weight,
    cache,
    select,
    hidden,
    gain,
    ffn_gain,
    conv_weight,
    conv_bias,
    step_bias,
    skip_gain,
    step_gain,
    decay,
    experts,
    share,
    in_weight_out,
    cache_out,
    select_out,
    hidden_out,
    gain_out,
    ffn_gain_out,
    columns,
    step_gain_out,
    rates,
    weights,
    conv_weight_in,
    conv_bias_in,
    step_bias_in,
    skip_gain_in,
    step_gain_in,
    decay_in,
    experts_in,
    share_in,
    packed,
    sems,
):
    small = start_copies(
        (
            (conv_weight, conv_weight_in),
            (conv_bias, conv_bias_in),
            (step_bias, step_bias_in),
            (skip_gain, skip_gain_in),
            (step_gain, step_gain_in),
            (decay, decay_in),
            (experts, experts_in),
            (share, share_in),
        ),
        sems,
    )
    large = start_copies(
        (
            (in_weight, in_weight_out),
            (cache, cache_out),
            (select, select_out),
            (hidden, hidden_out),
            (gain, gain_out),
            (ffn_gain, ffn_gain_out),
        ),
        sems.at[pl.ds(len(small), 6)],
    )
    finish(small)
    taps, channels = conv_weight.shape
    packed[...] = jnp.zeros(packed.shape, F32)
    packed[:taps, :channels] = conv_weight_in[...]
    packed[taps : taps + 1, :channels] = conv_bias_in[...]
    packed[taps + 1 : taps + 2, :channels] = step_bias_in[...]
    packed[taps + 2 : taps + 3, :channels] = skip_gain_in[...]
    columns[...] = packed[...].T[:channels, :]
    rank = step_gain.shape[1]
    packed[:1, :rank] = step_gain_in[...]
    step_gain_out[...] = packed[...].T[:rank, :]
    topk, count = experts.shape
    packed[:topk, :count] = f32(experts_in[...])
    packed[topk : 2 * topk, :count] = share_in[...]
    turned = packed[:, :LANES].T[:count, :]
    lane = lax.broadcasted_iota(jnp.int32, (count, LANES), 1)
    first = lane < LANES // 2
    number = f32(jnp.where(first, lane, lane - LANES // 2))
    dense = jnp.zeros(lane.shape, F32)
    for k in range(topk):
        hit = number == turned[:, k : k + 1]
        dense = dense + jnp.where(hit, turned[:, topk + k : topk + k + 1], 0.0)
    upper = dense.astype(BF16)
    lower = (dense - f32(upper)).astype(BF16)
    weights[...] = jnp.where(first, f32(upper), f32(lower)).astype(BF16)
    rate = -jnp.exp(decay_in[...])
    for c in range(channels):
        rates[c] = jnp.broadcast_to(rate[:, c : c + 1], rates.shape[1:])
    finish(large)


def project_kernel(blocks, *refs):
    rows = refs[:blocks]
    gain, weight, cache, columns, select = refs[blocks : blocks + 5]
    conved_out, normed, keep, send, selected = refs[blocks + 5 :]
    me = lax.axis_index("wide")
    count = rows[0].shape[0]
    for j in range(blocks):
        start = pl.multiple_of((me ^ j) * count, count)
        normed[pl.ds(start, count), :] = normalized(rows[j][...], gain[...])
    dims = (((1,), (1,)), ((), ()))
    x_input = lax.dot_general(weight[0], normed[...], dims, preferred_element_type=F32)
    pre_conv = columns[:, 4:5] + columns[:, 3:4] * x_input
    for tap in range(3):
        pre_conv = pre_conv + columns[:, tap : tap + 1] * f32(cache[tap])
    conved = sigmoid_times(pre_conv)
    conved_out[...] = conved
    selected[...] = jnp.dot(select[...], conved.astype(BF16), preferred_element_type=F32)
    half = keep.shape[0]
    side = me & 1
    keep[...] = selected[pl.ds(pl.multiple_of(side * half, 16), half), :].astype(BF16)
    send[...] = selected[pl.ds(pl.multiple_of((1 - side) * half, 16), half), :].astype(BF16)


def gate_kernel(weight, normed, out):
    dims = (((1,), (1,)), ((), ()))
    z_gate = lax.dot_general(weight[1], normed[...], dims, preferred_element_type=F32)
    out[...] = sigmoid_times(z_gate)


def state_kernel(
    blocks,
    own_half,
    other_half,
    step_gain,
    step_weight,
    columns,
    conved,
    gate,
    cache,
    rates,
    out_weight,
    new_state,
    keep,
    send,
    selected,
    step,
    driven,
    mixed,
    turned,
):
    me = lax.axis_index("wide")
    side = me & 1
    half = own_half.shape[0]
    channels, states, rows = cache.shape
    rank = step_weight.shape[1]
    count = rows // blocks
    selected[pl.ds(pl.multiple_of(side * half, 16), half), :] = f32(own_half[...])
    selected[pl.ds(pl.multiple_of((1 - side) * half, 16), half), :] = f32(other_half[...])
    low = selected[:rank, :]
    mean_square = jnp.mean(low * low, axis=0, keepdims=True)
    step_low = (low * lax.rsqrt(mean_square + EPS) * step_gain[:, :1]).astype(BF16)
    raw = jnp.dot(step_weight[...], step_low, preferred_element_type=F32) + columns[:, 5:6]
    sizes = jnp.maximum(raw, 0.0) + jnp.log1p(jnp.exp(-jnp.abs(raw)))
    step[...] = sizes
    driven[...] = sizes * conved[...]
    in_coef = selected[rank : rank + states, :]
    out_coef = selected[rank + states :, :]

    def channel(c, carry):
        one = pl.ds(c, 1)
        state = jnp.exp(step[one, :] * rates[c]) * f32(cache[c]) + driven[one, :] * in_coef
        new_state[c] = state.astype(BF16)
        mixed[one, :] = jnp.sum(state * out_coef, axis=0, keepdims=True)
        return carry

    lax.fori_loop(0, channels, channel, 0, unroll=8)
    gated = (mixed[...] + columns[:, 6:7] * conved[...]) * gate[...]
    turned[...] = gated.T
    parts = []
    for side_of in range(2):
        for k in range(blocks // 2):
            start = pl.multiple_of((me ^ (2 * k + side_of)) * count, count)
            parts.append(turned[pl.ds(start, count), :].astype(BF16))
    left = jnp.concatenate(parts, axis=0)
    kept = keep.shape[0]
    width = out_weight.shape[1]
    piece = 512 if width % 512 == 0 else width
    for start in range(0, width, piece):
        span = slice(start, start + piece)
        partial = jnp.dot(left, out_weight[:, span], preferred_element_type=F32).astype(BF16)
        keep[:, span] = partial[:kept]
        send[:, span] = partial[kept:]


def split_kernel(keep, got, *outs):
    count = outs[0].shape[0]
    for k, out in enumerate(outs):
        span = slice(k * count, (k + 1) * count)
        out[...] = (f32(keep[span, :]) + f32(got[span, :])).astype(BF16)


def add_kernel(count, *refs):
    total = f32(refs[0][...])
    for ref in refs[1:count]:
        total = total + f32(ref[...])
    refs[-1][...] = total.astype(refs[-1].dtype)


def residual_kernel(mine, got, hidden, weights, out):
    width = hidden.shape[1]
    residual = f32(hidden[...]) + (f32(mine[...]) + f32(got[...]))
    out[:, :width] = residual.astype(BF16)
    out[:, width:] = weights[...]


def expert_kernel(blocks, steps, near_units, group, *refs):
    rows, refs = refs[:blocks], refs[blocks:]
    gain, downs, refs = refs[0], refs[1 : 1 + steps], refs[1 + steps :]
    lead = len(near_units)
    pairs_near, refs = dict(zip(near_units, refs[:lead])), refs[lead:]
    gate_proj, up_proj, keep, send, normed, share, total, pairs, sems = refs
    count = rows[0].shape[0]
    width = gain.shape[1]
    size = pairs.shape[2] // 2
    units = gate_proj.shape[1] // size

    far_units = [i for i in range(units) if i not in near_units]

    def copies(n):
        slot = n % pairs.shape[0]
        span = pl.ds(far_units[n] * size, size)
        return [
            pltpu.make_async_copy(
                source.at[:, span], pairs.at[slot, :, pl.ds(which * size, size)], sems.at[slot, which]
            )
            for which, source in enumerate((gate_proj, up_proj))
        ]

    def begin(n):
        if n < len(far_units):
            for copy in copies(n):
                copy.start()

    for n in range(pairs.shape[0]):
        begin(n)
    expert = lax.axis_index("wide") // group
    lane = lax.broadcasted_iota(jnp.int32, (count, LANES), 1)
    wanted = (lane == expert) | (lane == expert + LANES // 2)
    for j in range(blocks):
        span = slice(j * count, (j + 1) * count)
        normed[span, :] = normalized(rows[j][:, :width], gain[...])
        shares = jnp.where(wanted, f32(rows[j][:, width:]), 0.0)
        share[span, :] = jnp.broadcast_to(jnp.sum(shares, axis=1, keepdims=True), (count, LANES))

    def inner_of(pair):
        both = jnp.dot(normed[...], pair, preferred_element_type=F32)
        return (sigmoid_times(both[:, :size]) * both[:, size:]).astype(BF16)

    for step, down in enumerate(downs):
        inner = []
        for i in range(step * units // steps, (step + 1) * units // steps):
            if i in pairs_near:
                inner.append(inner_of(pairs_near[i][...]))
            else:
                n = far_units.index(i)
                finish(copies(n))
                inner.append(inner_of(pairs[n % pairs.shape[0]]))
                begin(n + pairs.shape[0])
        inner = jnp.concatenate(inner, axis=1)
        added = jnp.dot(inner, down[...], preferred_element_type=F32)
        if step:
            total[...] += added
        else:
            total[...] = added
    weighted = (total[...] * share[:, :1]).astype(BF16)
    kept = keep.shape[0]
    keep[...] = weighted[:kept]
    send[...] = weighted[kept:]


def columns_kernel(narrow_count, *refs):
    ins, outs = refs[:-narrow_count], refs[-narrow_count:]
    size = outs[0].shape[1]
    for me in range(narrow_count):

        @pl.when(lax.axis_index("narrow") == me)
        def _(me=me):
            for k, out in enumerate(outs):
                first = (me ^ k) * size
                span = slice(first, first + size)
                total = f32(ins[0][:, span])
                for ref in ins[1:]:
                    total = total + f32(ref[:, span])
                out[...] = total.astype(BF16)


def final_kernel(narrow_count, residual, *refs):
    *ins, out = refs
    size = out.shape[1]
    for me in range(narrow_count):

        @pl.when(lax.axis_index("narrow") == me)
        def _(me=me):
            total = f32(ins[0][...])
            for ref in ins[1:]:
                total = total + f32(ref[...])
            out[...] = (f32(residual[:, me * size : (me + 1) * size]) + total).astype(BF16)


def on_device(
    hidden,
    conv_cache,
    ssm_cache,
    mixer_gain,
    in_weight,
    conv_weight,
    conv_bias,
    select_weight,
    step_gain,
    step_weight,
    step_bias,
    decay_log,
    skip_gain,
    out_weight,
    ffn_gain,
    gate_proj,
    up_proj,
    down_proj,
    route_experts,
    route_share,
):
    narrow_count = lax.axis_size("narrow")
    wide_count = lax.axis_size("wide")
    chips = wide_count // 2
    count, width = hidden.shape
    rows = count * wide_count
    channels, states = decay_log.shape
    chosen = select_weight.shape[1]
    hidden_units = gate_proj.shape[1]

    def swap(values):
        return lax.ppermute(values, "wide", [(i, i ^ 1) for i in range(wide_count)])

    def to_chip(values, k):
        return lax.ppermute(values, "wide", [(i, i ^ (2 * k)) for i in range(wide_count)])

    def to_narrow(values, k):
        return lax.ppermute(values, "narrow", [(i, i ^ k) for i in range(narrow_count)])

    def fetch_rows(start, number, after, *stored):
        outs = [((block, width), BF16)] * number
        outs += [(item.shape, item.dtype) for item in stored]
        *got, token = kernel_call(
            functools.partial(fetch_rows_kernel, start * block, len(stored)),
            [*outs, ((8, LANES), F32)],
            (after, *stored, down_proj),
            far=1,
            scratch=[pltpu.SemaphoreType.DMA((number * PIECES + len(stored),))],
            cost=pl.CostEstimate(
                flops=0, bytes_accessed=4 * number * block * width, transcendentals=0
            ),
            far_outs=range(number, number + len(stored)),
        )
        return got[:number], token, got[number:]

    def fetch_columns(chosen_units, after):
        if not chosen_units:
            return [], after
        number = len(chosen_units)
        *got, again = kernel_call(
            functools.partial(fetch_columns_kernel, [i * unit for i in chosen_units]),
            [((width, 2 * unit), BF16)] * number + [(after.shape, BF16)],
            (after, gate_proj, up_proj),
            far=2,
            scratch=[pltpu.SemaphoreType.DMA((2 * number,))],
            cost=pl.CostEstimate(
                flops=0, bytes_accessed=8 * number * unit * width, transcendentals=0
            ),
        )
        return got, again

    def plane_gather(block, near):
        same = [near, *[to_chip(block, k) for k in range(1, chips)]]
        other = [swap(item) for item in same]
        return same, other

    def plane_scatter(keep, got):
        return kernel_call(split_kernel, [((count, width), BF16)] * chips, (keep, got))

    def to_chips(parts):
        return [to_chip(parts[k], k) for k in range(1, chips)]

    def add(*items, token=None):
        args = items if token is None else (*items, token)
        body = functools.partial(add_kernel, len(items))
        return kernel_call(body, [(items[0].shape, BF16)], args)[0]

    block = next(size for size in (512, 256, 128, hidden_units) if hidden_units % size == 0)
    steps = hidden_units // block
    third = max(1, steps // 3)
    unit = block // 2 if block % (2 * LANES) == 0 else block
    units = hidden_units // unit
    lead = units // 6
    near_units = tuple(i * units // lead for i in range(lead))
    lead_first = 2 * lead // 3
    rank = step_weight.shape[1]
    topk = route_experts.shape[1]
    padded = max(LANES, channels, rank)
    (
        in_weight_near,
        conv_cache_near,
        select_near,
        hidden_near,
        mixer_gain_near,
        ffn_gain_near,
        columns,
        step_gain_column,
        rates,
        weights,
    ) = kernel_call(
        stage_kernel,
        [
            (in_weight.shape, BF16),
            (conv_cache.shape, BF16),
            ((chosen, channels), BF16),
            (hidden.shape, BF16),
            ((1, width), F32),
            ((1, width), F32),
            ((channels, LANES), F32),
            ((rank, LANES), F32),
            ((channels, states, rows), F32),
            ((count, LANES), BF16),
        ],
        (
            in_weight,
            conv_cache,
            select_weight.T,
            hidden,
            mixer_gain[None, :],
            ffn_gain[None, :],
            conv_weight,
            conv_bias[None, :],
            step_bias[None, :],
            skip_gain[None, :],
            step_gain[None, :],
            decay_log.T,
            route_experts.T,
            route_share.T,
        ),
        far=14,
        scratch=[
            pltpu.VMEM(conv_weight.shape, F32),
            pltpu.VMEM((1, channels), F32),
            pltpu.VMEM((1, channels), F32),
            pltpu.VMEM((1, channels), F32),
            pltpu.VMEM((1, rank), F32),
            pltpu.VMEM((states, channels), F32),
            pltpu.VMEM((topk, count), jnp.int32),
            pltpu.VMEM((topk, count), F32),
            pltpu.VMEM((LANES, padded), F32),
            pltpu.SemaphoreType.DMA((14,)),
        ],
        limit=16,
        cost=pl.CostEstimate(
            flops=0,
            bytes_accessed=4 * in_weight.size,
            transcendentals=decay_log.size,
        ),
    )

    same, other = plane_gather(hidden, hidden_near)
    interleaved = [item for pair in zip(same, other) for item in pair]
    half = chosen // 2
    conved, normed, keep, send = kernel_call(
        functools.partial(project_kernel, wide_count),
        [
            ((channels, rows), F32),
            ((rows, width), BF16),
            ((half, rows), BF16),
            ((half, rows), BF16),
        ],
        (
            *interleaved,
            mixer_gain_near,
            in_weight_near,
            conv_cache_near,
            columns,
            select_near,
        ),
        scratch=[pltpu.VMEM((chosen, rows), F32)],
        limit=16,
    )
    part = add(keep, swap(send))
    (gate,) = kernel_call(
        gate_kernel,
        [((channels, rows), F32)],
        (in_weight_near, normed),
        limit=8,
        cost=pl.CostEstimate(
            flops=2 * channels * width * rows,
            bytes_accessed=2 * in_weight.size,
            transcendentals=channels * rows,
        ),
    )
    out_weight_near, step_weight_near, states_near, token = kernel_call(
        fetch_kernel,
        [
            (out_weight.shape, BF16),
            (step_weight.shape, BF16),
            (ssm_cache.shape, BF16),
            ((8, LANES), F32),
        ],
        (part, out_weight, step_weight, ssm_cache),
        far=3,
        scratch=[pltpu.SemaphoreType.DMA((3,))],
        cost=pl.CostEstimate(
            flops=0, bytes_accessed=4 * (out_weight.size + ssm_cache.size), transcendentals=0
        ),
    )
    part = add(part, *[to_chip(part, k) for k in range(1, chips)], token=token)
    down_first, token, _ = fetch_rows(0, third, part)
    part = add(part, *[to_narrow(part, k) for k in range(1, narrow_count)], token=token)
    new_state_near, keep, send = kernel_call(
        functools.partial(state_kernel, wide_count),
        [
            (ssm_cache.shape, BF16),
            ((rows // 2, width), BF16),
            ((rows // 2, width), BF16),
        ],
        (
            part,
            swap(part),
            step_gain_column,
            step_weight_near,
            columns,
            conved,
            gate,
            states_near,
            rates,
            out_weight_near,
        ),
        scratch=[
            pltpu.VMEM((chosen, rows), F32),
            pltpu.VMEM((channels, rows), F32),
            pltpu.VMEM((channels, rows), F32),
            pltpu.VMEM((channels, rows), F32),
            pltpu.VMEM((rows, channels), F32),
        ],
        limit=16,
    )
    parts = plane_scatter(keep, swap(send))
    down_second, token, (new_state,) = fetch_rows(third, third, parts[0], new_state_near)
    mine = add(parts[0], *to_chips(parts), token=token)
    down_third, token, _ = fetch_rows(2 * third, steps - 2 * third, mine)
    step = 1
    while 2 * step < narrow_count:
        mine = add(mine, to_narrow(mine, step), token=token)
        step *= 2
    pairs_first, again = fetch_columns(near_units[:lead_first], mine)
    (residual,) = kernel_call(
        residual_kernel,
        [((count, width + LANES), BF16)],
        (again, to_narrow(mine, step), hidden_near, weights),
    )
    pairs_second, again = fetch_columns(near_units[lead_first:], residual)
    same, other = plane_gather(residual, again)
    keep, send = kernel_call(
        functools.partial(expert_kernel, wide_count, steps, near_units, wide_count // EXPERTS),
        [((rows // 2, width), BF16)] * 2,
        (
            *same,
            *other,
            ffn_gain_near,
            *down_first,
            *down_second,
            *down_third,
            *pairs_first,
            *pairs_second,
            gate_proj,
            up_proj,
        ),
        far=2,
        scratch=[
            pltpu.VMEM((rows, width), BF16),
            pltpu.VMEM((rows, LANES), F32),
            pltpu.VMEM((rows, width), F32),
            pltpu.VMEM((3, width, 2 * unit), BF16),
            pltpu.SemaphoreType.DMA((3, 2)),
        ],
        limit=18 if rows <= 256 else 24,
    )
    parts = plane_scatter(keep, swap(send))
    parts = [parts[0], *to_chips(parts)]
    col_share = width // narrow_count
    shares = kernel_call(
        functools.partial(columns_kernel, narrow_count),
        [((count, col_share), BF16)] * narrow_count, parts
    )
    (layer_out,) = kernel_call(
        functools.partial(final_kernel, narrow_count),
        [((count, col_share), BF16)],
        (
            residual,
            shares[0],
            *[to_narrow(shares[k], k) for k in range(1, narrow_count)],
        ),
    )
    return (layer_out, new_state)


def solution(mesh):
    placed = (
        P("wide", None),
        P(None, ("wide", "narrow"), None),
        P(("wide", "narrow"), None, None),
        P(),
        P(None, ("wide", "narrow"), None),
        P(None, ("wide", "narrow")),
        P(("wide", "narrow")),
        P(("wide", "narrow"), None),
        P(),
        P(("wide", "narrow"), None),
        P(("wide", "narrow")),
        P(("wide", "narrow"), None),
        P(("wide", "narrow")),
        P(("wide", "narrow"), None),
        P(),
        P(None, ("wide", "narrow")),
        P(None, ("wide", "narrow")),
        P(("wide", "narrow"), None),
        P("wide", None),
        P("wide", None),
    )
    return jax.shard_map(
        on_device,
        mesh=mesh,
        in_specs=placed,
        out_specs=(P("wide", "narrow"), P(("wide", "narrow"), None, None)),
        check_vma=False,
    )
```

```python
import functools

import jax
import jax.numpy as jnp
from jax import lax
from jax.experimental import pallas as pl
from jax.experimental.pallas import tpu as pltpu
from jax.sharding import PartitionSpec as P

EXPERTS = 8
EPS = 1e-06
MIB = 1 << 20
LANES = 128
PIECES = 2
F32 = jnp.float32
BF16 = jnp.bfloat16


def f32(values):
    return values.astype(F32)


def kernel_call(body, outs, args, far=0, scratch=(), limit=2, cost=None, far_outs=()):
    vmem = pl.BlockSpec(memory_space=pltpu.VMEM)
    hbm = pl.BlockSpec(memory_space=pltpu.HBM)
    near = len(args) - far
    stay = [pltpu.with_memory_space_constraint(item, pltpu.HBM) for item in args[near:]]
    args = (*args[:near], *stay)
    return pl.pallas_call(
        body,
        out_shape=[jax.ShapeDtypeStruct(*out) for out in outs],
        in_specs=[vmem] * near + [hbm] * far,
        out_specs=[hbm if i in far_outs else vmem for i in range(len(outs))],
        scratch_shapes=scratch,
        compiler_params=pltpu.CompilerParams(vmem_limit_bytes=limit * MIB),
        cost_estimate=cost,
    )(*args)


def start_copies(pairs, sems):
    copies = [pltpu.make_async_copy(src, dst, sems.at[i]) for i, (src, dst) in enumerate(pairs)]
    for copy in copies:
        copy.start()
    return copies


def finish(copies):
    for copy in copies:
        copy.wait()


def fetch_rows_kernel(start, stores, after, *refs):
    stored, (source, *outs), (token, sems) = refs[:stores], refs[stores:-2], refs[-2:]
    stored_out, outs = outs[len(outs) - stores :], outs[: len(outs) - stores]
    size = outs[0].shape[0] // PIECES
    pairs = list(zip(stored, stored_out))
    for i, out in enumerate(outs):
        for j in range(PIECES):
            first = start + (i * PIECES + j) * size
            pairs.append((source.at[pl.ds(first, size), :], out.at[pl.ds(j * size, size), :]))
    copies = start_copies(pairs, sems)
    token[...] = jnp.zeros(token.shape, F32)
    finish(copies)


def fetch_kernel(after, first, second, third, first_out, second_out, third_out, token, sems):
    copies = start_copies(((first, first_out), (second, second_out), (third, third_out)), sems)
    token[...] = jnp.zeros(token.shape, F32)
    finish(copies)


def fetch_columns_kernel(starts, block, first, second, *refs):
    *outs, block_out, sems = refs
    size = outs[0].shape[1] // 2
    pairs = []
    for start, out in zip(starts, outs, strict=True):
        span = pl.ds(start, size)
        pairs.append((first.at[:, span], out.at[:, pl.ds(0, size)]))
        pairs.append((second.at[:, span], out.at[:, pl.ds(size, size)]))
    copies = start_copies(pairs, sems)
    block_out[...] = block[...]
    finish(copies)


def normalized(block, gain):
    values = f32(block)
    mean_square = jnp.mean(values * values, axis=-1, keepdims=True)
    return (values * lax.rsqrt(mean_square + EPS) * gain).astype(BF16)


def sigmoid_times(values):
    return values / (1.0 + jnp.exp(-values))


def stage_kernel(
    in_weight,
    cache,
    select,
    hidden,
    gain,
    ffn_gain,
    conv_weight,
    conv_bias,
    step_bias,
    skip_gain,
    step_gain,
    decay,
    experts,
    share,
    in_weight_out,
    cache_out,
    select_out,
    hidden_out,
    gain_out,
    ffn_gain_out,
    columns,
    step_gain_out,
    rates,
    weights,
    conv_weight_in,
    conv_bias_in,
    step_bias_in,
    skip_gain_in,
    step_gain_in,
    decay_in,
    experts_in,
    share_in,
    packed,
    sems,
):
    small = start_copies(
        (
            (conv_weight, conv_weight_in),
            (conv_bias, conv_bias_in),
            (step_bias, step_bias_in),
            (skip_gain, skip_gain_in),
            (step_gain, step_gain_in),
            (decay, decay_in),
            (experts, experts_in),
            (share, share_in),
        ),
        sems,
    )
    large = start_copies(
        (
            (in_weight, in_weight_out),
            (cache, cache_out),
            (select, select_out),
            (hidden, hidden_out),
            (gain, gain_out),
            (ffn_gain, ffn_gain_out),
        ),
        sems.at[pl.ds(len(small), 6)],
    )
    finish(small)
    taps, channels = conv_weight.shape
    packed[...] = jnp.zeros(packed.shape, F32)
    packed[:taps, :channels] = conv_weight_in[...]
    packed[taps : taps + 1, :channels] = conv_bias_in[...]
    packed[taps + 1 : taps + 2, :channels] = step_bias_in[...]
    packed[taps + 2 : taps + 3, :channels] = skip_gain_in[...]
    columns[...] = packed[...].T[:channels, :]
    rank = step_gain.shape[1]
    packed[:1, :rank] = step_gain_in[...]
    step_gain_out[...] = packed[...].T[:rank, :]
    topk, count = experts.shape
    packed[:topk, :count] = f32(experts_in[...])
    packed[topk : 2 * topk, :count] = share_in[...]
    turned = packed[:, :LANES].T[:count, :]
    lane = lax.broadcasted_iota(jnp.int32, (count, LANES), 1)
    first = lane < LANES // 2
    number = f32(jnp.where(first, lane, lane - LANES // 2))
    dense = jnp.zeros(lane.shape, F32)
    for k in range(topk):
        hit = number == turned[:, k : k + 1]
        dense = dense + jnp.where(hit, turned[:, topk + k : topk + k + 1], 0.0)
    upper = dense.astype(BF16)
    lower = (dense - f32(upper)).astype(BF16)
    weights[...] = jnp.where(first, f32(upper), f32(lower)).astype(BF16)
    rate = -jnp.exp(decay_in[...])
    for c in range(channels):
        rates[c] = jnp.broadcast_to(rate[:, c : c + 1], rates.shape[1:])
    finish(large)


def project_kernel(blocks, *refs):
    rows = refs[:blocks]
    gain, weight, cache, columns, select = refs[blocks : blocks + 5]
    conved_out, normed, keep, send, selected = refs[blocks + 5 :]
    me = lax.axis_index("wide")
    count = rows[0].shape[0]
    for j in range(blocks):
        start = pl.multiple_of((me ^ j) * count, count)
        normed[pl.ds(start, count), :] = normalized(rows[j][...], gain[...])
    dims = (((1,), (1,)), ((), ()))
    x_input = lax.dot_general(weight[0], normed[...], dims, preferred_element_type=F32)
    pre_conv = columns[:, 4:5] + columns[:, 3:4] * x_input
    for tap in range(3):
        pre_conv = pre_conv + columns[:, tap : tap + 1] * f32(cache[tap])
    conved = sigmoid_times(pre_conv)
    conved_out[...] = conved
    selected[...] = jnp.dot(select[...], conved.astype(BF16), preferred_element_type=F32)
    half = keep.shape[0]
    side = me & 1
    keep[...] = selected[pl.ds(pl.multiple_of(side * half, 16), half), :].astype(BF16)
    send[...] = selected[pl.ds(pl.multiple_of((1 - side) * half, 16), half), :].astype(BF16)


def gate_kernel(weight, normed, out):
    dims = (((1,), (1,)), ((), ()))
    z_gate = lax.dot_general(weight[1], normed[...], dims, preferred_element_type=F32)
    out[...] = sigmoid_times(z_gate)


def state_kernel(
    blocks,
    own_half,
    other_half,
    step_gain,
    step_weight,
    columns,
    conved,
    gate,
    cache,
    rates,
    out_weight,
    new_state,
    keep,
    send,
    selected,
    step,
    driven,
    mixed,
    turned,
):
    me = lax.axis_index("wide")
    side = me & 1
    half = own_half.shape[0]
    channels, states, rows = cache.shape
    rank = step_weight.shape[1]
    count = rows // blocks
    selected[pl.ds(pl.multiple_of(side * half, 16), half), :] = f32(own_half[...])
    selected[pl.ds(pl.multiple_of((1 - side) * half, 16), half), :] = f32(other_half[...])
    low = selected[:rank, :]
    mean_square = jnp.mean(low * low, axis=0, keepdims=True)
    step_low = (low * lax.rsqrt(mean_square + EPS) * step_gain[:, :1]).astype(BF16)
    raw = jnp.dot(step_weight[...], step_low, preferred_element_type=F32) + columns[:, 5:6]
    sizes = jnp.maximum(raw, 0.0) + jnp.log1p(jnp.exp(-jnp.abs(raw)))
    step[...] = sizes
    driven[...] = sizes * conved[...]
    in_coef = selected[rank : rank + states, :]
    out_coef = selected[rank + states :, :]

    def channel(c, carry):
        one = pl.ds(c, 1)
        state = jnp.exp(step[one, :] * rates[c]) * f32(cache[c]) + driven[one, :] * in_coef
        new_state[c] = state.astype(BF16)
        mixed[one, :] = jnp.sum(state * out_coef, axis=0, keepdims=True)
        return carry

    lax.fori_loop(0, channels, channel, 0, unroll=32)
    gated = (mixed[...] + columns[:, 6:7] * conved[...]) * gate[...]
    turned[...] = gated.T
    parts = []
    for side_of in range(2):
        for k in range(blocks // 2):
            start = pl.multiple_of((me ^ (2 * k + side_of)) * count, count)
            parts.append(turned[pl.ds(start, count), :].astype(BF16))
    left = jnp.concatenate(parts, axis=0)
    kept = keep.shape[0]
    width = out_weight.shape[1]
    piece = 512 if width % 512 == 0 else width
    for start in range(0, width, piece):
        span = slice(start, start + piece)
        partial = jnp.dot(left, out_weight[:, span], preferred_element_type=F32).astype(BF16)
        keep[:, span] = partial[:kept]
        send[:, span] = partial[kept:]


def split_kernel(keep, got, *outs):
    count = outs[0].shape[0]
    for k, out in enumerate(outs):
        span = slice(k * count, (k + 1) * count)
        out[...] = (f32(keep[span, :]) + f32(got[span, :])).astype(BF16)


def add_kernel(count, *refs):
    total = f32(refs[0][...])
    for ref in refs[1:count]:
        total = total + f32(ref[...])
    refs[-1][...] = total.astype(refs[-1].dtype)


def residual_kernel(mine, got, hidden, weights, out):
    width = hidden.shape[1]
    residual = f32(hidden[...]) + (f32(mine[...]) + f32(got[...]))
    out[:, :width] = residual.astype(BF16)
    out[:, width:] = weights[...]


def expert_kernel(blocks, steps, near_units, group, *refs):
    rows, refs = refs[:blocks], refs[blocks:]
    gain, downs, refs = refs[0], refs[1 : 1 + steps], refs[1 + steps :]
    lead = len(near_units)
    pairs_near, refs = dict(zip(near_units, refs[:lead])), refs[lead:]
    gate_proj, up_proj, keep, send, normed, share, total, pairs, sems = refs
    count = rows[0].shape[0]
    width = gain.shape[1]
    size = pairs.shape[2] // 2
    units = gate_proj.shape[1] // size

    far_units = [i for i in range(units) if i not in near_units]

    def copies(n):
        slot = n % pairs.shape[0]
        span = pl.ds(far_units[n] * size, size)
        return [
            pltpu.make_async_copy(
                source.at[:, span], pairs.at[slot, :, pl.ds(which * size, size)], sems.at[slot, which]
            )
            for which, source in enumerate((gate_proj, up_proj))
        ]

    def begin(n):
        if n < len(far_units):
            for copy in copies(n):
                copy.start()

    for n in range(pairs.shape[0]):
        begin(n)
    expert = lax.axis_index("wide") // group
    lane = lax.broadcasted_iota(jnp.int32, (count, LANES), 1)
    wanted = (lane == expert) | (lane == expert + LANES // 2)
    for j in range(blocks):
        span = slice(j * count, (j + 1) * count)
        normed[span, :] = normalized(rows[j][:, :width], gain[...])
        shares = jnp.where(wanted, f32(rows[j][:, width:]), 0.0)
        share[span, :] = jnp.broadcast_to(jnp.sum(shares, axis=1, keepdims=True), (count, LANES))

    def inner_of(pair):
        both = jnp.dot(normed[...], pair, preferred_element_type=F32)
        return (sigmoid_times(both[:, :size]) * both[:, size:]).astype(BF16)

    for step, down in enumerate(downs):
        inner = []
        for i in range(step * units // steps, (step + 1) * units // steps):
            if i in pairs_near:
                inner.append(inner_of(pairs_near[i][...]))
            else:
                n = far_units.index(i)
                finish(copies(n))
                inner.append(inner_of(pairs[n % pairs.shape[0]]))
                begin(n + pairs.shape[0])
        inner = jnp.concatenate(inner, axis=1)
        added = jnp.dot(inner, down[...], preferred_element_type=F32)
        if step:
            total[...] += added
        else:
            total[...] = added
    weighted = (total[...] * share[:, :1]).astype(BF16)
    kept = keep.shape[0]
    keep[...] = weighted[:kept]
    send[...] = weighted[kept:]


def columns_kernel(narrow_count, *refs):
    ins, outs = refs[:-narrow_count], refs[-narrow_count:]
    size = outs[0].shape[1]
    for me in range(narrow_count):

        @pl.when(lax.axis_index("narrow") == me)
        def _(me=me):
            for k, out in enumerate(outs):
                first = (me ^ k) * size
                span = slice(first, first + size)
                total = f32(ins[0][:, span])
                for ref in ins[1:]:
                    total = total + f32(ref[:, span])
                out[...] = total.astype(BF16)


def final_kernel(narrow_count, residual, *refs):
    *ins, out = refs
    size = out.shape[1]
    for me in range(narrow_count):

        @pl.when(lax.axis_index("narrow") == me)
        def _(me=me):
            total = f32(ins[0][...])
            for ref in ins[1:]:
                total = total + f32(ref[...])
            out[...] = (f32(residual[:, me * size : (me + 1) * size]) + total).astype(BF16)


def on_device(
    hidden,
    conv_cache,
    ssm_cache,
    mixer_gain,
    in_weight,
    conv_weight,
    conv_bias,
    select_weight,
    step_gain,
    step_weight,
    step_bias,
    decay_log,
    skip_gain,
    out_weight,
    ffn_gain,
    gate_proj,
    up_proj,
    down_proj,
    route_experts,
    route_share,
):
    narrow_count = lax.axis_size("narrow")
    wide_count = lax.axis_size("wide")
    chips = wide_count // 2
    count, width = hidden.shape
    rows = count * wide_count
    channels, states = decay_log.shape
    chosen = select_weight.shape[1]
    hidden_units = gate_proj.shape[1]

    def swap(values):
        return lax.ppermute(values, "wide", [(i, i ^ 1) for i in range(wide_count)])

    def to_chip(values, k):
        return lax.ppermute(values, "wide", [(i, i ^ (2 * k)) for i in range(wide_count)])

    def to_narrow(values, k):
        return lax.ppermute(values, "narrow", [(i, i ^ k) for i in range(narrow_count)])

    def fetch_rows(start, number, after, *stored):
        outs = [((block, width), BF16)] * number
        outs += [(item.shape, item.dtype) for item in stored]
        *got, token = kernel_call(
            functools.partial(fetch_rows_kernel, start * block, len(stored)),
            [*outs, ((8, LANES), F32)],
            (after, *stored, down_proj),
            far=1,
            scratch=[pltpu.SemaphoreType.DMA((number * PIECES + len(stored),))],
            cost=pl.CostEstimate(
                flops=0, bytes_accessed=4 * number * block * width, transcendentals=0
            ),
            far_outs=range(number, number + len(stored)),
        )
        return got[:number], token, got[number:]

    def fetch_columns(chosen_units, after):
        if not chosen_units:
            return [], after
        number = len(chosen_units)
        *got, again = kernel_call(
            functools.partial(fetch_columns_kernel, [i * unit for i in chosen_units]),
            [((width, 2 * unit), BF16)] * number + [(after.shape, BF16)],
            (after, gate_proj, up_proj),
            far=2,
            scratch=[pltpu.SemaphoreType.DMA((2 * number,))],
            cost=pl.CostEstimate(
                flops=0, bytes_accessed=8 * number * unit * width, transcendentals=0
            ),
        )
        return got, again

    def plane_gather(block, near):
        same = [near, *[to_chip(block, k) for k in range(1, chips)]]
        other = [swap(item) for item in same]
        return same, other

    def plane_scatter(keep, got):
        return kernel_call(split_kernel, [((count, width), BF16)] * chips, (keep, got))

    def to_chips(parts):
        return [to_chip(parts[k], k) for k in range(1, chips)]

    def add(*items, token=None):
        args = items if token is None else (*items, token)
        body = functools.partial(add_kernel, len(items))
        return kernel_call(body, [(items[0].shape, BF16)], args)[0]

    block = next(size for size in (512, 256, 128, hidden_units) if hidden_units % size == 0)
    steps = hidden_units // block
    third = max(1, steps // 3)
    unit = block // 2 if block % (2 * LANES) == 0 else block
    units = hidden_units // unit
    lead = units // 6
    near_units = tuple(i * units // lead for i in range(lead))
    lead_first = 2 * lead // 3
    rank = step_weight.shape[1]
    topk = route_experts.shape[1]
    padded = max(LANES, channels, rank)
    (
        in_weight_near,
        conv_cache_near,
        select_near,
        hidden_near,
        mixer_gain_near,
        ffn_gain_near,
        columns,
        step_gain_column,
        rates,
        weights,
    ) = kernel_call(
        stage_kernel,
        [
            (in_weight.shape, BF16),
            (conv_cache.shape, BF16),
            ((chosen, channels), BF16),
            (hidden.shape, BF16),
            ((1, width), F32),
            ((1, width), F32),
            ((channels, LANES), F32),
            ((rank, LANES), F32),
            ((channels, states, rows), F32),
            ((count, LANES), BF16),
        ],
        (
            in_weight,
            conv_cache,
            select_weight.T,
            hidden,
            mixer_gain[None, :],
            ffn_gain[None, :],
            conv_weight,
            conv_bias[None, :],
            step_bias[None, :],
            skip_gain[None, :],
            step_gain[None, :],
            decay_log.T,
            route_experts.T,
            route_share.T,
        ),
        far=14,
        scratch=[
            pltpu.VMEM(conv_weight.shape, F32),
            pltpu.VMEM((1, channels), F32),
            pltpu.VMEM((1, channels), F32),
            pltpu.VMEM((1, channels), F32),
            pltpu.VMEM((1, rank), F32),
            pltpu.VMEM((states, channels), F32),
            pltpu.VMEM((topk, count), jnp.int32),
            pltpu.VMEM((topk, count), F32),
            pltpu.VMEM((LANES, padded), F32),
            pltpu.SemaphoreType.DMA((14,)),
        ],
        limit=16,
        cost=pl.CostEstimate(
            flops=0,
            bytes_accessed=4 * in_weight.size,
            transcendentals=decay_log.size,
        ),
    )

    same, other = plane_gather(hidden, hidden_near)
    interleaved = [item for pair in zip(same, other) for item in pair]
    half = chosen // 2
    conved, normed, keep, send = kernel_call(
        functools.partial(project_kernel, wide_count),
        [
            ((channels, rows), F32),
            ((rows, width), BF16),
            ((half, rows), BF16),
            ((half, rows), BF16),
        ],
        (
            *interleaved,
            mixer_gain_near,
            in_weight_near,
            conv_cache_near,
            columns,
            select_near,
        ),
        scratch=[pltpu.VMEM((chosen, rows), F32)],
        limit=16,
    )
    part = add(keep, swap(send))
    (gate,) = kernel_call(
        gate_kernel,
        [((channels, rows), F32)],
        (in_weight_near, normed),
        limit=8,
        cost=pl.CostEstimate(
            flops=2 * channels * width * rows,
            bytes_accessed=2 * in_weight.size,
            transcendentals=channels * rows,
        ),
    )
    out_weight_near, step_weight_near, states_near, token = kernel_call(
        fetch_kernel,
        [
            (out_weight.shape, BF16),
            (step_weight.shape, BF16),
            (ssm_cache.shape, BF16),
            ((8, LANES), F32),
        ],
        (part, out_weight, step_weight, ssm_cache),
        far=3,
        scratch=[pltpu.SemaphoreType.DMA((3,))],
        cost=pl.CostEstimate(
            flops=0, bytes_accessed=4 * (out_weight.size + ssm_cache.size), transcendentals=0
        ),
    )
    part = add(part, *[to_chip(part, k) for k in range(1, chips)], token=token)
    down_first, token, _ = fetch_rows(0, third, part)
    part = add(part, *[to_narrow(part, k) for k in range(1, narrow_count)], token=token)
    new_state_near, keep, send = kernel_call(
        functools.partial(state_kernel, wide_count),
        [
            (ssm_cache.shape, BF16),
            ((rows // 2, width), BF16),
            ((rows // 2, width), BF16),
        ],
        (
            part,
            swap(part),
            step_gain_column,
            step_weight_near,
            columns,
            conved,
            gate,
            states_near,
            rates,
            out_weight_near,
        ),
        scratch=[
            pltpu.VMEM((chosen, rows), F32),
            pltpu.VMEM((channels, rows), F32),
            pltpu.VMEM((channels, rows), F32),
            pltpu.VMEM((channels, rows), F32),
            pltpu.VMEM((rows, channels), F32),
        ],
        limit=16,
    )
    parts = plane_scatter(keep, swap(send))
    down_second, token, (new_state,) = fetch_rows(third, third, parts[0], new_state_near)
    mine = add(parts[0], *to_chips(parts), token=token)
    down_third, token, _ = fetch_rows(2 * third, steps - 2 * third, mine)
    step = 1
    while 2 * step < narrow_count:
        mine = add(mine, to_narrow(mine, step), token=token)
        step *= 2
    pairs_first, again = fetch_columns(near_units[:lead_first], mine)
    (residual,) = kernel_call(
        residual_kernel,
        [((count, width + LANES), BF16)],
        (again, to_narrow(mine, step), hidden_near, weights),
    )
    pairs_second, again = fetch_columns(near_units[lead_first:], residual)
    same, other = plane_gather(residual, again)
    keep, send = kernel_call(
        functools.partial(expert_kernel, wide_count, steps, near_units, wide_count // EXPERTS),
        [((rows // 2, width), BF16)] * 2,
        (
            *same,
            *other,
            ffn_gain_near,
            *down_first,
            *down_second,
            *down_third,
            *pairs_first,
            *pairs_second,
            gate_proj,
            up_proj,
        ),
        far=2,
        scratch=[
            pltpu.VMEM((rows, width), BF16),
            pltpu.VMEM((rows, LANES), F32),
            pltpu.VMEM((rows, width), F32),
            pltpu.VMEM((3, width, 2 * unit), BF16),
            pltpu.SemaphoreType.DMA((3, 2)),
        ],
        limit=18 if rows <= 256 else 24,
    )
    parts = plane_scatter(keep, swap(send))
    parts = [parts[0], *to_chips(parts)]
    col_share = width // narrow_count
    shares = kernel_call(
        functools.partial(columns_kernel, narrow_count),
        [((count, col_share), BF16)] * narrow_count, parts
    )
    (layer_out,) = kernel_call(
        functools.partial(final_kernel, narrow_count),
        [((count, col_share), BF16)],
        (
            residual,
            shares[0],
            *[to_narrow(shares[k], k) for k in range(1, narrow_count)],
        ),
    )
    return (layer_out, new_state)


def solution(mesh):
    placed = (
        P("wide", None),
        P(None, ("wide", "narrow"), None),
        P(("wide", "narrow"), None, None),
        P(),
        P(None, ("wide", "narrow"), None),
        P(None, ("wide", "narrow")),
        P(("wide", "narrow")),
        P(("wide", "narrow"), None),
        P(),
        P(("wide", "narrow"), None),
        P(("wide", "narrow")),
        P(("wide", "narrow"), None),
        P(("wide", "narrow")),
        P(("wide", "narrow"), None),
        P(),
        P(None, ("wide", "narrow")),
        P(None, ("wide", "narrow")),
        P(("wide", "narrow"), None),
        P("wide", None),
        P("wide", None),
    )
    return jax.shard_map(
        on_device,
        mesh=mesh,
        in_specs=placed,
        out_specs=(P("wide", "narrow"), P(("wide", "narrow"), None, None)),
        check_vma=False,
    )
```
